256 devices in a mesh: space: 16 (over y_hi, x, core), batch: 16 (over z, y_lo).
Axes of the slice: x: 4, y: 4 (y_hi: 2, y_lo: 2; y = y_hi * 2 + y_lo), z: 8, core: 2. Of those that a mesh axis runs over, the one named last changes fastest.
Arguments:
- inputs: bfloat16 [16, 112, 7, 7, 1024], P('batch', 'space'), may hold values from -60 to 60
- grad_out: bfloat16 [16, 112, 7, 7, 1024], P('batch', 'space'), may hold values from -6 to 6
- fluid: int32 [112, 7, 7], P('space'), may hold values 0 or 1
- w_qkv: bfloat16 [1024, 3072], P('batch')
- qkv_bias: float32 [3072], replicated, may hold values from -3 to 3
- w_proj: bfloat16 [1024, 1024], P('batch'), may hold values from -0.1875 to 0.1875
- ln_gain: float32 [1024], replicated, may hold values from 0.5 to 1.5
Outputs:
- grad_input: bfloat16 [16, 112, 7, 7, 1024], P('batch', 'space')
- grad_qkv: float32 [1024, 3072], P('batch')
- grad_proj: float32 [1024, 1024], P('batch')
- grad_gain: float32 [1024], replicated
- grad_bias: float32 [3072], replicated
The draws below stay inside these ranges and needn't reach their ends.
All inputs are finite; a program needn't handle non-finite values. No bound on the sum of `fluid` on one device may be relied on, other than what follows from the above.
Results may differ from the reference program's by a relative error of at most 0.03.
Values may be sent and summed in bfloat16 or wider, within the bound.
No kernel may reach another device: no remote copies, remote signals or barrier semaphores. Data moves between devices by JAX's collectives and lax.ppermute only.
A program may use at most 128 MiB of HBM per device.

```python
import math
import jax
import jax.numpy as jnp
from jax import lax

C = 1024
HD = 64
WIN = 7
SHIFT = 3
SNAP_DEV = 1
SNAPS = 16
NX1 = 112
N_SPACE = 16
N_BATCH = 16


def draw_inputs(key, part):
    key = jax.random.fold_in(key, 5)
    first, second = jax.random.split(key, 2)
    shape = (SNAPS, NX1, WIN, WIN, C)
    scales = jnp.exp(jax.random.uniform(second, shape[:-1] + (1,), minval=0.0, maxval=2.3))
    raw = jax.random.normal(first, shape)
    return (jnp.clip(raw, -6.0, 6.0) * scales).astype(jnp.bfloat16)


def draw_w_qkv(key, part):
    key = jax.random.fold_in(key, 11)
    first = jax.random.fold_in(key, 0)
    base = jnp.clip(jax.random.normal(first, (C, 3 * C)), -6.0, 6.0) * C ** (-0.5)
    return base.astype(jnp.bfloat16)


def with_ends(entries, rng, least, largest):
    longest = entries.shape.index(max(entries.shape))
    spots = []
    for shift in (0, 1):
        where = [jax.random.randint(jax.random.fold_in(rng, axis), (), 0, length) for axis, length in enumerate(entries.shape)]
        where[longest] = (where[longest] + shift) % entries.shape[longest]
        spots.append(tuple(where))
    return entries.at[spots[0]].set(least).at[spots[1]].set(largest)


def levels(stream_key, dims, cuts, smallest, largest):
    gain = 1.0
    for axis_at, shards_of in cuts:
        steps = jax.random.uniform(jax.random.fold_in(jax.random.fold_in(stream_key, 6), axis_at), (shards_of,), jnp.float32, smallest / len(cuts), largest / len(cuts))
        gain = gain * jnp.repeat(jnp.exp(steps), dims[axis_at] // shards_of).reshape((-1,) + (1,) * (len(dims) - 1 - axis_at))
    return gain


def scatter_about(key, shape, scale, reach, pieces=(), held_as=jnp.bfloat16):
    result = jax.random.normal(key, shape, jnp.float32) * scale
    if len(pieces) > 0:
        result = levels(key, shape, pieces, -0.22, 0.18) * result
    return jnp.clip(result, min=-reach, max=reach).astype(held_as)


def setup_inputs(seed: int = 0) -> dict:
    streams_of = jax.random.split(jax.random.key(seed), 8)
    inputs = draw_inputs(jax.random.fold_in(streams_of[7], 71), 0)
    grad_out = scatter_about(streams_of[1], (SNAPS, NX1, WIN, WIN, C), 1.0, 6.0, ((0, 16), (1, 16)))
    fluid = with_ends((jax.random.randint(streams_of[2], (NX1, WIN, WIN), 0, 4) < 3).astype(jnp.int32), jax.random.fold_in(streams_of[2], 1), 0, 1)
    w_qkv = draw_w_qkv(jax.random.fold_in(streams_of[7], 71), 0)
    qkv_bias = scatter_about(streams_of[4], (3 * C,), 0.5, 3.0, (), jnp.float32)
    w_proj = scatter_about(streams_of[5], (C, C), C ** -0.5, 0.1875, ((0, 16),))
    ln_gain = jnp.clip(1.0 + 0.1 * jax.random.normal(streams_of[6], (C,), jnp.float32), 0.5, 1.5)
    return dict(inputs=inputs, grad_out=grad_out, fluid=fluid, w_qkv=w_qkv, qkv_bias=qkv_bias, w_proj=w_proj, ln_gain=ln_gain)


EPS = 1e-05
NEG = -1e+30
heads_per_block = 4

def rounded(value):
    return lax.optimization_barrier(value.astype(jnp.bfloat16)).astype(jnp.float32)

def region(extent):
    places = jnp.arange(extent, dtype=jnp.int32)
    return jnp.where(places < extent - WIN, 0, jnp.where(places < extent - SHIFT, 1, 2)).astype(jnp.int32)

def attend_block(queries, keys, values, dout, allowed):
    scale = 1.0 / math.sqrt(HD)
    full = jnp.float32
    scores = jnp.einsum('sqhd,skhd->shqk', queries.astype(full), keys.astype(full)) * scale
    scores = jnp.where(allowed[None, None], scores, NEG)
    maxima = lax.optimization_barrier(jnp.max(scores, -1, keepdims=True))
    exponent = jnp.exp(scores - maxima)
    probability = exponent / lax.optimization_barrier(jnp.sum(exponent, -1, keepdims=True))
    prob_low = probability.astype(jnp.bfloat16)
    attended = jnp.einsum('shqk,skhd->sqhd', prob_low.astype(full), values.astype(full)).astype(jnp.bfloat16)
    grad_prob = jnp.einsum('sqhd,skhd->shqk', dout.astype(full), values.astype(full))
    grad_score = probability * (grad_prob - lax.optimization_barrier(jnp.sum(probability * grad_prob, -1, keepdims=True)))
    score_low = grad_score.astype(jnp.bfloat16).astype(full)
    grad_q = (jnp.einsum('shqk,skhd->sqhd', score_low, keys.astype(full)) * scale).astype(jnp.bfloat16)
    grad_k = (jnp.einsum('shqk,sqhd->skhd', score_low, queries.astype(full)) * scale).astype(jnp.bfloat16)
    grad_v = jnp.einsum('shqk,sqhd->skhd', prob_low.astype(full), dout.astype(full)).astype(jnp.bfloat16)
    return (attended, grad_q, grad_k, grad_v)

def split_heads(block):
    snaps, tokens, width = block.shape
    grouped = block.reshape(snaps, tokens, width // (heads_per_block * HD), heads_per_block, HD)
    return grouped.transpose(2, 0, 1, 3, 4)

def join_heads(block):
    groups, snaps, tokens, heads, size = block.shape
    return block.transpose(1, 2, 0, 3, 4).reshape(snaps, tokens, groups * heads * size)

def tile_pass(tile_x, tile_g, allowed, w_qkv, qkv_bias, w_proj, ln_gain):
    snaps, tokens, width = tile_x.shape
    flat_x = tile_x.reshape(-1, width).astype(jnp.float32)
    average = lax.optimization_barrier(jnp.mean(flat_x, -1, keepdims=True))
    centred = flat_x - average
    variance = lax.optimization_barrier(jnp.mean(centred * centred, -1, keepdims=True))
    inv_std = 1.0 / jnp.sqrt(variance + EPS)
    normed = centred * inv_std
    hidden = (normed * ln_gain).astype(jnp.bfloat16)
    qkv = (jnp.dot(hidden, w_qkv, preferred_element_type=jnp.float32) + qkv_bias).astype(jnp.bfloat16)
    flat_g = tile_g.reshape(-1, width)
    dout = lax.dot_general(flat_g, w_proj, (((1,), (1,)), ((), ())), preferred_element_type=jnp.float32).astype(jnp.bfloat16)
    shaped = qkv.reshape(snaps, tokens, 3 * width)
    parts = (split_heads(shaped[:, :, :width]), split_heads(shaped[:, :, width:2 * width]), split_heads(shaped[:, :, 2 * width:]), split_heads(dout.reshape(snaps, tokens, width)))
    attended, grad_q, grad_k, grad_v = lax.map(lambda items: attend_block(items[0], items[1], items[2], items[3], allowed), parts)
    attn_flat = join_heads(attended).reshape(-1, width)
    grad_qkv = jnp.concatenate([join_heads(grad_q), join_heads(grad_k), join_heads(grad_v)], -1).reshape(-1, 3 * width)
    grad_hidden = lax.dot_general(grad_qkv, w_qkv, (((1,), (1,)), ((), ())), preferred_element_type=jnp.float32)
    gain_term = lax.optimization_barrier(jnp.sum(grad_hidden * normed, 0))
    bias_term = lax.optimization_barrier(jnp.sum(grad_qkv.astype(jnp.float32), 0))
    grad_norm = grad_hidden * ln_gain
    grad_flat = flat_g.astype(jnp.float32) + inv_std * (grad_norm - lax.optimization_barrier(jnp.mean(grad_norm, -1, keepdims=True)) - normed * lax.optimization_barrier(jnp.mean(grad_norm * normed, -1, keepdims=True)))
    return (grad_flat.astype(jnp.bfloat16).reshape(tile_x.shape), hidden, grad_qkv, attn_flat, flat_g, gain_term, bias_term)

def reference(inputs, grad_out, fluid, w_qkv, qkv_bias, w_proj, ln_gain):
    tokens = WIN ** 3
    shifted_x = jnp.roll(inputs, (-SHIFT, -SHIFT, -SHIFT), (1, 2, 3))
    shifted_g = jnp.roll(grad_out, (-SHIFT, -SHIFT, -SHIFT), (1, 2, 3))
    shifted_f = jnp.roll(fluid, (-SHIFT, -SHIFT, -SHIFT), (0, 1, 2))
    tiles_x = shifted_x.reshape(N_BATCH, SNAP_DEV, N_SPACE, tokens, C).transpose(0, 2, 1, 3, 4).reshape(N_BATCH * N_SPACE, SNAP_DEV, tokens, C)
    tiles_g = shifted_g.reshape(N_BATCH, SNAP_DEV, N_SPACE, tokens, C).transpose(0, 2, 1, 3, 4).reshape(N_BATCH * N_SPACE, SNAP_DEV, tokens, C)
    tiles_f = shifted_f.reshape(N_SPACE, tokens)
    long_labels = region(NX1).reshape(N_SPACE, WIN)
    inner = region(WIN)
    diagonal = jnp.eye(tokens, dtype=bool)

    def visit(carry, index):
        tile = index % N_SPACE
        along = long_labels[tile]
        labels = (along[:, None, None] * 9 + inner[None, :, None] * 3 + inner[None, None, :]).reshape(-1)
        walls = tiles_f[tile]
        allowed = (labels[:, None] == labels[None, :]) & ((walls[None, :] == 1) | diagonal)
        grad_tile, hidden, grad_qkv, attn_flat, flat_g, gain_term, bias_term = tile_pass(tiles_x[index], tiles_g[index], allowed, w_qkv, qkv_bias, w_proj, ln_gain)
        term = rounded(jnp.concatenate([jnp.dot(hidden.T, grad_qkv, preferred_element_type=jnp.float32), jnp.dot(attn_flat.T, flat_g, preferred_element_type=jnp.float32)], 1))
        return ((carry[0] + term, carry[1] + gain_term, carry[2] + bias_term), grad_tile)
    start = (jnp.zeros((C, 4 * C), jnp.float32), jnp.zeros((C,), jnp.float32), jnp.zeros((3 * C,), jnp.float32))
    totals, grad_tiles = lax.scan(visit, start, jnp.arange(N_BATCH * N_SPACE, dtype=jnp.int32))
    grad_shifted = grad_tiles.reshape(N_BATCH, N_SPACE, SNAP_DEV, tokens, C).transpose(0, 2, 1, 3, 4).reshape(SNAPS, NX1, WIN, WIN, C)
    grad_input = jnp.roll(grad_shifted, (SHIFT, SHIFT, SHIFT), (1, 2, 3))
    return (grad_input, totals[0][:, :3 * C], totals[0][:, 3 * C:], totals[1], totals[2])
```

```python
import itertools
import math

import jax
import jax.numpy as jnp
from jax import lax
from jax.experimental import pallas as pl
from jax.experimental.pallas import tpu as pltpu
from jax.sharding import PartitionSpec as P

HEADS = 16
WIN = 7
SHIFT = 3
TOKENS = WIN**3
ROWS = 352
EPS = 1e-05
NEG = -1e30
BOTH = ("space", "batch")
SIZE = {"x": 4, "y": 4, "z": 8, "c": 2}
ORDER = "xyzc"


def flat(x, y, z, c):
    return ((y // 2 * 4 + x) * 2 + c) * 16 + z * 2 + y % 2


def places():
    s, b = lax.axis_index("space"), lax.axis_index("batch")
    return {"x": s // 2 % 4, "y": s // 8 * 2 + b % 2, "z": b // 2, "c": s % 2}


def move(block, axis, distance):
    route = []
    for at in itertools.product(*(range(SIZE[name]) for name in ORDER)):
        to = list(at)
        index = ORDER.index(axis)
        to[index] = (to[index] + distance) % SIZE[axis]
        route.append((flat(*at), flat(*to)))
    return lax.ppermute(block, BOTH, route)


def swap(block):
    return move(block, "c", 1)


def spread(block, axis, me, shape, spot):
    n = SIZE[axis]
    whole = jnp.zeros(shape, block.dtype)
    incoming = [block] + [move(block, axis, d) for d in range(1, n)]
    for d, piece in enumerate(incoming):
        start = spot((me[axis] - d) % n)
        extent = [1 if isinstance(i, jax.Array) else length for i, length in zip(start, shape)]
        whole = lax.dynamic_update_slice(whole, piece.reshape(extent), start)
    return whole


def reduce_to(block, axis, me, spot):
    n = SIZE[axis]

    def piece(coordinate):
        start = spot(coordinate)
        extent = [
            1 if isinstance(i, jax.Array) else length for i, length in zip(start, block.shape)
        ]
        kept = [l for i, l in zip(start, block.shape) if not isinstance(i, jax.Array)]
        return lax.dynamic_slice(block, start, extent).reshape(kept)

    total = piece(me[axis]).astype(jnp.float32)
    for d in range(1, n):
        total = total + move(piece((me[axis] + d) % n), axis, d).astype(jnp.float32)
    return total.astype(block.dtype)


def attention_kernel(q_ref, k_ref, v_ref, g_ref, mask_ref, attn_ref, dq_ref, dk_ref, dv_ref):
    full = jnp.float32
    size = 64
    scale = 1.0 / math.sqrt(size)
    over_rows = (((0,), (0,)), ((), ()))
    over_columns = (((1,), (1,)), ((), ()))
    mask = mask_ref[0]
    for head in range(2):
        part = slice(head * size, (head + 1) * size)
        q, k, v, g = q_ref[:, part], k_ref[:, part], v_ref[:, part], g_ref[:, part]
        scores = lax.dot_general(k, q, over_columns, preferred_element_type=full) * scale + mask
        exponent = jnp.exp(scores - jnp.max(scores, 0, keepdims=True))
        probability = exponent * (1.0 / jnp.sum(exponent, 0, keepdims=True))
        low = probability.astype(jnp.bfloat16)
        grad = lax.dot_general(v, g, over_columns, preferred_element_type=full)
        centre = jnp.sum(probability * grad, 0, keepdims=True)
        score_low = (probability * (grad - centre)).astype(jnp.bfloat16)
        attn_ref[:, part] = lax.dot_general(
            low, v, over_rows, preferred_element_type=full
        ).astype(jnp.bfloat16)
        dq_ref[:, part] = (
            lax.dot_general(score_low, k, over_rows, preferred_element_type=full) * scale
        ).astype(jnp.bfloat16)
        dk_ref[:, part] = (jnp.dot(score_low, q, preferred_element_type=full) * scale).astype(
            jnp.bfloat16
        )
        dv_ref[:, part] = jnp.dot(low, g, preferred_element_type=full).astype(jnp.bfloat16)


def attend(qkv, dout, mask):
    rows, width = dout.shape
    pairs = width // 128

    def columns(offset):
        return pl.BlockSpec((ROWS, 128), lambda w, j: (w, offset + j))

    shape = jax.ShapeDtypeStruct((rows, width), jnp.bfloat16)
    work = 2 * pairs * 2
    return pl.pallas_call(
        attention_kernel,
        grid=(2, pairs),
        in_specs=[
            columns(0),
            columns(pairs),
            columns(2 * pairs),
            columns(0),
            pl.BlockSpec((1, ROWS, ROWS), lambda w, j: (w, 0, 0)),
        ],
        out_specs=[columns(0)] * 4,
        out_shape=[shape] * 4,
        cost_estimate=pl.CostEstimate(
            flops=work * 14 * ROWS * ROWS * 64 * 4,
            bytes_accessed=8 * rows * width * 2,
            transcendentals=work * ROWS * ROWS,
        ),
        compiler_params=pltpu.CompilerParams(vmem_limit_bytes=32 * 2**20),
    )(qkv, qkv, qkv, dout, mask)


def per_device(inputs, grad_out, fluid, w_qkv, qkv_bias, w_proj, ln_gain):
    full, low = jnp.float32, jnp.bfloat16
    width = w_proj.shape[1]
    half = width // 2
    me = places()
    core = me["c"]
    first = core == 0
    own_rows = w_qkv.shape[0]
    portion = own_rows // 8

    qkv_parts = w_qkv.reshape(own_rows, 3, 2, half)
    mine = jnp.concatenate(
        [
            jnp.where(first, qkv_parts[:, i, 0], qkv_parts[:, i, 1]) for i in range(3)
        ] + [jnp.where(first, w_proj[:, :half], w_proj[:, half:])],
        1,
    )
    zero = 0
    share = lax.dynamic_slice(
        mine, ((me["y"] // 2 * 4 + me["x"]) * portion, 0), (portion, 2 * width)
    )
    lined = spread(share, "z", me, (8, portion, 2 * width), lambda z: (z, zero, zero))
    on_y = spread(
        lined[:, :, :width], "y", me, (8, 2, 2, portion, width),
        lambda y: (zero, y % 2, y // 2, zero, zero),
    )
    on_x = spread(
        lined[:, :, width:], "x", me, (8, 4, portion, width),
        lambda x: (zero, x, zero, zero),
    )
    whole = (8, 2, 2, 4, portion, width)
    w_qk = spread(
        on_y, "x", me, whole, lambda x: (zero, zero, zero, x, zero, zero)
    ).reshape(width, width)
    w_vp = spread(
        on_x, "y", me, whole, lambda y: (zero, y % 2, y // 2, zero, zero, zero)
    ).reshape(width, width)
    w_v = w_vp[:, :half]
    proj_half = w_vp[:, half:]
    kept = jnp.where(first, proj_half[:half], proj_half[half:])
    got = swap(jnp.where(first, proj_half[half:], proj_half[:half]))
    proj_rows = jnp.where(
        first, jnp.concatenate([kept, got], 1), jnp.concatenate([got, kept], 1)
    )

    def back(block):
        n = lax.axis_size("space")
        return lax.ppermute(block, "space", [((i + 1) % n, i) for i in range(n)])

    rim_x, rim_g, rim_f = (back(block) for block in (inputs[:, :SHIFT], grad_out[:, :SHIFT], fluid[:SHIFT]))
    tile_x = jnp.roll(jnp.concatenate([inputs[:, SHIFT:], rim_x], 1), (-SHIFT, -SHIFT), (2, 3))
    tile_g = jnp.roll(jnp.concatenate([grad_out[:, SHIFT:], rim_g], 1), (-SHIFT, -SHIFT), (2, 3))
    tile_f = jnp.roll(jnp.concatenate([fluid[SHIFT:], rim_f], 0), (-SHIFT, -SHIFT), (1, 2))
    other_f = swap(tile_f)
    extra = ((0, ROWS - TOKENS), (0, 0))
    flat_x = jnp.pad(tile_x.reshape(-1, width), extra).astype(full)
    flat_g = jnp.pad(tile_g.reshape(-1, width), extra)
    average = jnp.mean(flat_x, -1, keepdims=True)
    centred = flat_x - average
    variance = jnp.mean(centred * centred, -1, keepdims=True)
    inv_std = 1.0 / jnp.sqrt(variance + EPS)
    normed = centred * inv_std
    hidden = (normed * ln_gain).astype(low)
    hiddens = jnp.concatenate([hidden, swap(hidden)], 0)
    grads = jnp.concatenate([flat_g, swap(flat_g)], 0)

    steps = jnp.arange(WIN, dtype=jnp.int32)
    inner = jnp.where(steps < WIN - SHIFT, 1, 2).astype(jnp.int32)
    last_pair = (me["x"] == 3) & (me["y"] >= 2)

    def masked(walls, is_last):
        along = jnp.where(is_last, inner, 0)
        labels = along[:, None, None] * 9 + inner[None, :, None] * 3 + inner[None, None, :]
        labels = jnp.pad(labels.reshape(-1), (0, ROWS - TOKENS), constant_values=-1)
        open_keys = jnp.pad(walls.reshape(-1) == 1, (0, ROWS - TOKENS))
        allowed = (labels[:, None] == labels[None, :]) & (
            open_keys[:, None] | jnp.eye(ROWS, dtype=bool)
        )
        return jnp.where(allowed, 0.0, NEG).astype(full)

    mask = jnp.stack(
        [
            masked(tile_f, last_pair & (core == 1)),
            masked(other_f, last_pair & (core == 0)),
        ]
    )

    biases = qkv_bias.reshape(3, 2, half)
    biases = jnp.where(first, biases[:, 0], biases[:, 1]).reshape(-1)
    qkv = jnp.concatenate(
        [
            jnp.dot(hiddens, w_qk, preferred_element_type=full),
            jnp.dot(hiddens, w_v, preferred_element_type=full),
        ],
        1,
    )
    qkv = (qkv + biases).astype(low)
    dout = lax.dot_general(
        grads, proj_rows, (((1,), (1,)), ((), ())), preferred_element_type=full
    ).astype(low)
    attn, grad_q, grad_k, grad_v = attend(qkv, dout, mask)

    def over_tokens(left, right):
        return lax.dot_general(
            left, right, (((0,), (0,)), ((), ())), preferred_element_type=full
        ).astype(low)

    proj_terms = over_tokens(attn, grads)
    term_got = swap(jnp.where(first, proj_terms[:, half:], proj_terms[:, :half]))
    term_kept = jnp.where(first, proj_terms[:, :half], proj_terms[:, half:])
    proj_column = jnp.where(
        first, jnp.concatenate([term_kept, term_got], 0), jnp.concatenate([term_got, term_kept], 0)
    )
    term_qk = jnp.concatenate([over_tokens(hiddens, grad_q), over_tokens(hiddens, grad_k)], 1)
    term_vp = jnp.concatenate([over_tokens(hiddens, grad_v), proj_column], 1)
    sum_x = reduce_to(
        term_qk.reshape(whole), "x", me, lambda x: (zero, zero, zero, x, zero, zero)
    )
    sum_y = reduce_to(
        term_vp.reshape(whole), "y", me, lambda y: (zero, y % 2, y // 2, zero, zero, zero)
    )
    sum_xy = reduce_to(sum_x, "y", me, lambda y: (zero, y % 2, y // 2, zero, zero))
    sum_yx = reduce_to(sum_y, "x", me, lambda x: (zero, x, zero, zero))
    sums = reduce_to(
        jnp.concatenate([sum_xy, sum_yx], -1), "z", me, lambda z: (z, zero, zero)
    )

    def cousin(block, dx, dy):
        n = lax.axis_size("space")
        route = [
            (i, ((i // 8 + dy) % 2 * 4 + (i // 2 + dx) % 4) * 2 + i % 2) for i in range(n)
        ]
        return lax.ppermute(block, "space", route)

    rows = jnp.zeros((2, 4, portion, 2 * width), low)
    for dy, dx in itertools.product(range(2), range(4)):
        piece = cousin(sums, dx, dy) if dx or dy else sums
        rows = lax.dynamic_update_slice(
            rows, piece[None, None], ((me["y"] // 2 + dy) % 2, (me["x"] - dx) % 4, zero, zero)
        )
    rows = rows.reshape(own_rows, 2 * width)
    others = swap(rows)
    sides = (jnp.where(first, rows, others), jnp.where(first, others, rows))
    joined = [
        side[:, i * half : (i + 1) * half].astype(full) for i in range(4) for side in sides
    ]
    out_qkv = jnp.concatenate(joined[:6], 1)
    out_proj = jnp.concatenate(joined[6:], 1)

    def back_through(grad, weight):
        return lax.dot_general(grad, weight, (((1,), (1,)), ((), ())), preferred_element_type=full)

    partial = (
        back_through(grad_q, w_qk[:, :half])
        + back_through(grad_k, w_qk[:, half:])
        + back_through(grad_v, w_v)
    )
    grad_hidden = partial[:ROWS] + swap(partial[ROWS:])
    grad_norm = grad_hidden * ln_gain
    grad_flat = flat_g.astype(full) + inv_std * (
        grad_norm
        - jnp.mean(grad_norm, -1, keepdims=True)
        - normed * jnp.mean(grad_norm * normed, -1, keepdims=True)
    )
    grad_tile = jnp.roll(
        grad_flat[:TOKENS].astype(low).reshape(tile_x.shape), (SHIFT, SHIFT), (2, 3)
    )
    n = lax.axis_size("space")
    returned = lax.ppermute(
        grad_tile[:, WIN - SHIFT :], "space", [(i, (i + 1) % n) for i in range(n)]
    )
    grad_input = jnp.concatenate([returned, grad_tile[:, : WIN - SHIFT]], 1)

    gain_term = jnp.sum(grad_hidden * normed, 0)
    nothing = jnp.zeros((half,), full)
    small = [gain_term]
    for grad in (grad_q, grad_k, grad_v):
        column = jnp.sum(grad, 0, dtype=full)
        small += [jnp.where(first, column, nothing), jnp.where(first, nothing, column)]
    small = jnp.concatenate(small).reshape(-1, 128)
    for axis in "cyxz":
        small = sum((move(small, axis, d) for d in range(1, SIZE[axis])), small)
    small = small.reshape(-1)
    return (grad_input, out_qkv, out_proj, small[:width], small[width:])


def solution(mesh):
    tokens = P("batch", "space", None, None, None)
    return jax.shard_map(
        per_device,
        mesh=mesh,
        in_specs=(tokens, tokens, P("space", None, None), P("batch", None), P(), P("batch", None), P()),
        out_specs=(tokens, P("batch", None), P("batch", None), P(), P()),
        check_vma=False,
    )
```

```python
import itertools
import math

import jax
import jax.numpy as jnp
from jax import lax
from jax.experimental import pallas as pl
from jax.experimental.pallas import tpu as pltpu
from jax.sharding import PartitionSpec as P

HEADS = 16
WIN = 7
SHIFT = 3
TOKENS = WIN**3
ROWS = 352
EPS = 1e-05
NEG = -1e30
BOTH = ("space", "batch")


def flat(x, y, z, c):
    return ((y // 2 * 4 + x) * 2 + c) * 16 + z * 2 + y % 2


def places():
    s, b = lax.axis_index("space"), lax.axis_index("batch")
    return {"x": s // 2 % 4, "y": s // 8 * 2 + b % 2, "z": b // 2, "c": s % 2}


def route(where):
    every = itertools.product(range(4), range(4), range(8), range(2))
    return [(flat(*at), flat(*where(*at))) for at in every]


def swap(block):
    return lax.ppermute(block, BOTH, route(lambda x, y, z, c: (x, y, z, 1 - c)))


def along_z(block, d):
    return lax.ppermute(block, BOTH, route(lambda x, y, z, c: (x, y, (z + d) % 8, c)))


def crossed(block, d, swapped):
    def where(x, y, z, c):
        if c == swapped:
            return ((x + d) % 4, y, z, c)
        return (x, (y + d) % 4, z, c)

    return lax.ppermute(block, BOTH, route(where))


def cousin(block, dx, dy):
    return lax.ppermute(
        block, BOTH, route(lambda x, y, z, c: ((x + dx) % 4, (y + 2 * dy) % 4, z, c))
    )


def at(array, index):
    return lax.dynamic_index_in_dim(array, index, 0, keepdims=False)


def attention_kernel(q_ref, k_ref, v_ref, g_ref, mask_ref, attn_ref, grad_ref):
    full = jnp.float32
    size = 64
    scale = 1.0 / math.sqrt(size)
    over_rows = (((0,), (0,)), ((), ()))
    over_columns = (((1,), (1,)), ((), ()))
    mask = mask_ref[0]
    for head in range(2):
        part = slice(head * size, (head + 1) * size)
        q, k, v, g = q_ref[:, part], k_ref[:, part], v_ref[:, part], g_ref[:, part]
        scores = lax.dot_general(k, q, over_columns, preferred_element_type=full) * scale + mask
        exponent = jnp.exp(scores - jnp.max(scores, 0, keepdims=True))
        probability = exponent * (1.0 / jnp.sum(exponent, 0, keepdims=True))
        low = probability.astype(jnp.bfloat16)
        grad = lax.dot_general(v, g, over_columns, preferred_element_type=full)
        centre = jnp.sum(probability * grad, 0, keepdims=True)
        score_low = (probability * (grad - centre)).astype(jnp.bfloat16)
        attn_ref[:, part] = lax.dot_general(
            low, v, over_rows, preferred_element_type=full
        ).astype(jnp.bfloat16)
        grad_ref[0, :, part] = (
            lax.dot_general(score_low, k, over_rows, preferred_element_type=full) * scale
        ).astype(jnp.bfloat16)
        grad_ref[1, :, part] = (jnp.dot(score_low, q, preferred_element_type=full) * scale).astype(
            jnp.bfloat16
        )
        grad_ref[2, :, part] = jnp.dot(low, g, preferred_element_type=full).astype(jnp.bfloat16)


def attend(qkv, dout, mask):
    rows, width = dout.shape
    pairs = width // 128

    def columns(offset):
        return pl.BlockSpec((ROWS, 128), lambda w, j: (w, offset + j))

    work = 2 * pairs * 2
    return pl.pallas_call(
        attention_kernel,
        grid=(2, pairs),
        in_specs=[
            columns(0),
            columns(pairs),
            columns(2 * pairs),
            columns(0),
            pl.BlockSpec((1, ROWS, ROWS), lambda w, j: (w, 0, 0)),
        ],
        out_specs=[columns(0), pl.BlockSpec((3, ROWS, 128), lambda w, j: (0, w, j))],
        out_shape=[
            jax.ShapeDtypeStruct((rows, width), jnp.bfloat16),
            jax.ShapeDtypeStruct((3, rows, width), jnp.bfloat16),
        ],
        cost_estimate=pl.CostEstimate(
            flops=work * 14 * ROWS * ROWS * 64 * 4,
            bytes_accessed=8 * rows * width * 2,
            transcendentals=work * ROWS * ROWS,
        ),
        compiler_params=pltpu.CompilerParams(vmem_limit_bytes=32 * 2**20),
    )(qkv, qkv, qkv, dout, mask)


LIMIT = pltpu.CompilerParams(vmem_limit_bytes=40 * 2**20)


def cost(flops, bytes_accessed):
    return pl.CostEstimate(flops=flops, bytes_accessed=bytes_accessed, transcendentals=0)


def project_kernel(hidden_ref, weight_ref, bias_ref, out_ref):
    out_ref[...] = (
        jnp.dot(hidden_ref[...], weight_ref[0], preferred_element_type=jnp.float32) + bias_ref[...]
    ).astype(jnp.bfloat16)


def project(hidden, weights, biases):
    rows, width = hidden.shape
    return pl.pallas_call(
        project_kernel,
        grid=(6,),
        in_specs=[
            pl.BlockSpec((rows, width), lambda i: (0, 0)),
            pl.BlockSpec((1, width, 256), lambda i: (i, 0, 0)),
            pl.BlockSpec((1, 256), lambda i: (0, i)),
        ],
        out_specs=pl.BlockSpec((rows, 256), lambda i: (0, i)),
        out_shape=jax.ShapeDtypeStruct((rows, 1536), jnp.bfloat16),
        cost_estimate=cost(2 * rows * width * 1536, 8 * 2**20),
        compiler_params=LIMIT,
    )(hidden, weights, biases)


def dout_kernel(grad_ref, kept_ref, got_ref, out_ref):
    total = 0.0
    for i, block in enumerate((kept_ref[0], kept_ref[1], got_ref[0], got_ref[1])):
        total = total + lax.dot_general(
            grad_ref[:, i * 256 : (i + 1) * 256],
            block,
            (((1,), (1,)), ((), ())),
            preferred_element_type=jnp.float32,
        )
    out_ref[...] = total.astype(jnp.bfloat16)


def find_dout(grads, kept, got):
    rows = grads.shape[0]
    return pl.pallas_call(
        dout_kernel,
        out_shape=jax.ShapeDtypeStruct((rows, 512), jnp.bfloat16),
        cost_estimate=cost(2 * rows * 1024 * 512, 4 * 2**20),
        compiler_params=LIMIT,
    )(grads, kept, got)


def terms_kernel(left_ref, right_ref, out_ref):
    out_ref[0] = jnp.dot(left_ref[...], right_ref[0], preferred_element_type=jnp.float32).astype(
        jnp.bfloat16
    )


def find_terms(hidden_t, grad_qkv):
    width, rows = hidden_t.shape
    return pl.pallas_call(
        terms_kernel,
        grid=(6,),
        in_specs=[
            pl.BlockSpec((width, rows), lambda i: (0, 0)),
            pl.BlockSpec((1, rows, 256), lambda i: (i // 2, 0, i % 2)),
        ],
        out_specs=pl.BlockSpec((1, width, 256), lambda i: (i, 0, 0)),
        out_shape=jax.ShapeDtypeStruct((8, width, 256), jnp.bfloat16),
        cost_estimate=cost(2 * rows * width * 1536, 8 * 2**20),
        compiler_params=LIMIT,
    )(hidden_t, grad_qkv)


def last_terms_kernel(left_ref, right_ref, terms_ref, out_ref):
    out_ref[0] = lax.dot_general(
        left_ref[...], right_ref[...], (((0,), (0,)), ((), ())), preferred_element_type=jnp.float32
    ).astype(jnp.bfloat16)


def add_last_terms(attn, grads, terms):
    rows, width = attn.shape
    return pl.pallas_call(
        last_terms_kernel,
        grid=(2,),
        in_specs=[
            pl.BlockSpec((rows, width), lambda i: (0, 0)),
            pl.BlockSpec((rows, 256), lambda i: (0, i)),
            pl.BlockSpec(memory_space=pl.ANY),
        ],
        out_specs=pl.BlockSpec((1, width, 256), lambda i: (6 + i, 0, 0)),
        out_shape=jax.ShapeDtypeStruct(terms.shape, terms.dtype),
        input_output_aliases={2: 0},
        cost_estimate=cost(2 * rows * width * 512, 4 * 2**20),
        compiler_params=LIMIT,
    )(attn, grads, terms)


def hidden_grad_kernel(grad_ref, weight_ref, normed_ref, out_ref, gain_ref, bias_ref):
    step = pl.program_id(0)
    grad = grad_ref[0]
    bias_ref[0] = jnp.sum(grad.astype(jnp.float32), 0, keepdims=True)
    part = lax.dot_general(
        grad, weight_ref[0], (((1,), (1,)), ((), ())), preferred_element_type=jnp.float32
    )

    @pl.when(step == 0)
    def _():
        out_ref[...] = part

    @pl.when(step > 0)
    def _():
        out_ref[...] += part

    @pl.when(step == 5)
    def _():
        gain_ref[...] = jnp.sum(out_ref[...] * normed_ref[...], 0, keepdims=True)


def find_hidden_grad(grad_qkv, weights, normed):
    rows, width = normed.shape
    return pl.pallas_call(
        hidden_grad_kernel,
        grid=(6,),
        in_specs=[
            pl.BlockSpec((1, rows, 256), lambda i: (i // 2, 0, i % 2)),
            pl.BlockSpec((1, width, 256), lambda i: (i, 0, 0)),
            pl.BlockSpec((rows, width), lambda i: (0, 0)),
        ],
        out_specs=[
            pl.BlockSpec((rows, width), lambda i: (0, 0)),
            pl.BlockSpec((1, width), lambda i: (0, 0)),
            pl.BlockSpec((1, 1, 256), lambda i: (i, 0, 0)),
        ],
        out_shape=[
            jax.ShapeDtypeStruct((rows, width), jnp.float32),
            jax.ShapeDtypeStruct((1, width), jnp.float32),
            jax.ShapeDtypeStruct((6, 1, 256), jnp.float32),
        ],
        cost_estimate=cost(2 * rows * width * 1536, 14 * 2**20),
        compiler_params=LIMIT,
    )(grad_qkv, weights, normed)


def per_device(inputs, grad_out, fluid, w_qkv, qkv_bias, w_proj, ln_gain):
    full, low = jnp.float32, jnp.bfloat16
    width = w_proj.shape[1]
    half = width // 2
    me = places()
    x, y, z, core = me["x"], me["y"], me["z"], me["c"]
    first = core == 0
    own_rows = w_qkv.shape[0]
    n_space = lax.axis_size("space")

    def block_of(x, y):
        return jnp.where(first, x * 2 + y // 2, y // 2 * 4 + x)

    def quarter_of(inner):
        return jnp.where(first, inner % 2 * 2 + inner // 2, inner)

    def pairs_of(outer):
        one = (jnp.where(first, outer, outer // 2 * 2), jnp.where(first, 0, outer % 2))
        two = (jnp.where(first, outer, outer // 2 * 2 + 1), jnp.where(first, 1, outer % 2))
        return one, two

    inner_at, outer_at = jnp.where(first, y, x), jnp.where(first, x, y)

    qkv_parts = w_qkv.reshape(own_rows, 3, 2, half)
    mine = jnp.concatenate(
        [jnp.where(first, qkv_parts[:, i, 0], qkv_parts[:, i, 1]) for i in range(3)]
        + [jnp.where(first, w_proj[:, :half], w_proj[:, half:])],
        1,
    )
    share = lax.dynamic_slice(mine, (0, block_of(x, y) * 256), (own_rows, 256))
    lined = jnp.zeros((8, own_rows, 256), low)
    for d in range(8):
        piece = along_z(share, d) if d else share
        lined = lax.dynamic_update_slice(lined, piece[None], ((z - d) % 8, 0, 0))
    quarters = jnp.zeros((4, 8, own_rows, 256), low)
    for d in range(4):
        piece = crossed(lined, d, 1) if d else lined
        quarters = lax.dynamic_update_slice(
            quarters, piece[None], (quarter_of((inner_at - d) % 4), 0, 0, 0)
        )
    weights = jnp.zeros((4, 2, 8, 2, own_rows, 256), low)
    for d in range(4):
        piece = crossed(quarters, d, 0) if d else quarters
        for i, (columns, low_y) in enumerate(pairs_of((outer_at - d) % 4)):
            weights = lax.dynamic_update_slice(
                weights,
                piece[2 * i : 2 * i + 2].reshape(1, 2, 8, 1, own_rows, 256),
                (columns, 0, 0, low_y, 0, 0),
            )
    weights = weights.reshape(8, width, 256)
    proj = weights[6:]
    kept = lax.dynamic_slice(proj, (0, core * half, 0), (2, half, 256))
    got = swap(lax.dynamic_slice(proj, (0, (1 - core) * half, 0), (2, half, 256)))

    def back(block):
        return lax.ppermute(block, "space", [((i + 1) % n_space, i) for i in range(n_space)])

    rim_x, rim_g, rim_f = (
        back(block) for block in (inputs[:, :SHIFT], grad_out[:, :SHIFT], fluid[:SHIFT])
    )
    tile_x = jnp.roll(jnp.concatenate([inputs[:, SHIFT:], rim_x], 1), (-SHIFT, -SHIFT), (2, 3))
    tile_g = jnp.roll(jnp.concatenate([grad_out[:, SHIFT:], rim_g], 1), (-SHIFT, -SHIFT), (2, 3))
    tile_f = jnp.roll(jnp.concatenate([fluid[SHIFT:], rim_f], 0), (-SHIFT, -SHIFT), (1, 2))
    other_f = swap(tile_f)
    extra = ((0, ROWS - TOKENS), (0, 0))
    rows_x = jnp.pad(tile_x.reshape(-1, width), extra)
    rows_g = jnp.pad(tile_g.reshape(-1, width), extra)
    both_x = jnp.concatenate([rows_x, swap(rows_x)], 0).astype(full)
    grads = jnp.concatenate([rows_g, swap(rows_g)], 0)
    average = jnp.mean(both_x, -1, keepdims=True)
    centred = both_x - average
    variance = jnp.mean(centred * centred, -1, keepdims=True)
    inv_std = 1.0 / jnp.sqrt(variance + EPS)
    normed = centred * inv_std
    hidden = (normed * ln_gain).astype(low)
    hidden_t = hidden.T
    grads_own_first = jnp.where(
        first, grads, jnp.concatenate([grads[:, half:], grads[:, :half]], 1)
    )

    steps = jnp.arange(WIN, dtype=jnp.int32)
    inner = jnp.where(steps < WIN - SHIFT, 1, 2).astype(jnp.int32)
    last_pair = (x == 3) & (y >= 2)

    def masked(walls, is_last):
        along = jnp.where(is_last, inner, 0)
        labels = along[:, None, None] * 9 + inner[None, :, None] * 3 + inner[None, None, :]
        labels = jnp.pad(labels.reshape(-1), (0, ROWS - TOKENS), constant_values=-1)
        open_keys = jnp.pad(walls.reshape(-1) == 1, (0, ROWS - TOKENS))
        allowed = (labels[:, None] == labels[None, :]) & (
            open_keys[:, None] | jnp.eye(ROWS, dtype=bool)
        )
        return jnp.where(allowed, 0.0, NEG).astype(full)

    mask = jnp.stack([masked(tile_f, last_pair & ~first), masked(other_f, last_pair & first)])

    biases = qkv_bias.reshape(3, 2, half)
    biases = jnp.where(first, biases[:, 0], biases[:, 1]).reshape(1, -1)
    qkv = project(hidden, weights, biases)
    dout = find_dout(grads_own_first, kept, got)
    attn, grad_qkv = attend(qkv, dout, mask)

    attn_got = swap(attn)
    attn_got = jnp.concatenate([attn_got[ROWS:], attn_got[:ROWS]], 0)
    attn_all = jnp.where(
        first, jnp.concatenate([attn, attn_got], 1), jnp.concatenate([attn_got, attn], 1)
    )
    terms = add_last_terms(attn_all, grads_own_first, find_terms(hidden_t, grad_qkv))
    terms = terms.reshape(4, 2, 8, 2, own_rows, 256)

    def outer_piece(coordinate):
        return jnp.concatenate(
            [
                lax.dynamic_slice(
                    terms, (columns, 0, 0, low_y, 0, 0), (1, 2, 8, 1, own_rows, 256)
                ).reshape(2, 8, own_rows, 256)
                for columns, low_y in pairs_of(coordinate)
            ],
            0,
        )

    sums = outer_piece(outer_at).astype(full)
    for d in range(1, 4):
        sums = sums + crossed(outer_piece((outer_at + d) % 4), d, 0).astype(full)
    sums = sums.astype(low)

    partial, gain_term, bias_term = find_hidden_grad(grad_qkv, weights, normed)
    bias_term = bias_term.reshape(3, 1, half)
    nothing = jnp.zeros_like(bias_term)
    bias_term = jnp.where(
        first,
        jnp.concatenate([bias_term, nothing], 1),
        jnp.concatenate([nothing, bias_term], 1),
    )
    small = jnp.concatenate([gain_term.reshape(-1), bias_term.reshape(-1)]).reshape(16, 256)
    small = small + swap(small)

    def split(values):
        upper = lax.reduce_precision(values, 8, 7)
        return jnp.concatenate([upper.astype(low), (values - upper).astype(low)], 0)

    def joined(rows):
        return rows[-32:-16].astype(full) + rows[-16:].astype(full)

    def with_small(rows, extra_rows):
        return jnp.concatenate([rows.reshape(-1, 256), extra_rows], 0)

    extra_rows = split(small)
    total = at(sums, quarter_of(inner_at)).reshape(-1, 256).astype(full)
    for d in range(1, 4):
        piece = at(sums, quarter_of((inner_at + d) % 4))
        arrived = crossed(with_small(piece, extra_rows), d, 1)
        total = total + arrived[:-32].astype(full)
        small = small + joined(arrived)
    sums = total.astype(low).reshape(8, own_rows, 256)
    extra_rows = split(small)
    total = at(sums, z).astype(full)
    for d in range(1, 8):
        arrived = along_z(with_small(at(sums, (z + d) % 8), extra_rows), d)
        total = total + arrived[:-32].astype(full)
        small = small + joined(arrived)
    extra_rows = split(small)
    final = with_small(total.astype(low), extra_rows)
    rows = jnp.zeros((8, own_rows, 256), low)
    for dy, dx in itertools.product(range(2), range(4)):
        piece = cousin(final, dx, dy) if dx or dy else final
        rows = lax.dynamic_update_slice(
            rows, piece[None, :own_rows], (block_of((x - dx) % 4, (y + 2 * dy) % 4), 0, 0)
        )
        if dx and not dy:
            small = small + joined(piece)
    others = swap(rows)
    small_got = swap(small)
    small = jnp.where(first, small, small_got).reshape(-1)
    sides = (jnp.where(first, rows, others), jnp.where(first, others, rows))
    blocks = [side[2 * i + j].astype(full) for i in range(4) for side in sides for j in range(2)]
    out_qkv = jnp.concatenate(blocks[:12], 1)
    out_proj = jnp.concatenate(blocks[12:], 1)

    grad_hidden = partial[:ROWS] + swap(partial[ROWS:])
    grad_norm = grad_hidden * ln_gain
    own_normed = normed[:ROWS]
    grad_flat = rows_g.astype(full) + inv_std[:ROWS] * (
        grad_norm
        - jnp.mean(grad_norm, -1, keepdims=True)
        - own_normed * jnp.mean(grad_norm * own_normed, -1, keepdims=True)
    )
    grad_tile = jnp.roll(
        grad_flat[:TOKENS].astype(low).reshape(tile_x.shape), (SHIFT, SHIFT), (2, 3)
    )
    returned = lax.ppermute(
        grad_tile[:, WIN - SHIFT :], "space", [(i, (i + 1) % n_space) for i in range(n_space)]
    )
    grad_input = jnp.concatenate([returned, grad_tile[:, : WIN - SHIFT]], 1)
    return (grad_input, out_qkv, out_proj, small[:width], small[width:])


def solution(mesh):
    tokens = P("batch", "space", None, None, None)
    return jax.shard_map(
        per_device,
        mesh=mesh,
        in_specs=(tokens, tokens, P("space", None, None), P("batch", None), P(), P("batch", None), P()),
        out_specs=(tokens, P("batch", None), P("batch", None), P(), P()),
        check_vma=False,
    )
```

```python
import itertools
import math

import jax
import jax.numpy as jnp
from jax import lax
from jax.experimental import pallas as pl
from jax.experimental.pallas import tpu as pltpu
from jax.sharding import PartitionSpec as P

HEADS = 16
WIN = 7
SHIFT = 3
TOKENS = WIN**3
ROWS = 352
EPS = 1e-05
NEG = -1e30
BOTH = ("space", "batch")


def flat(x, y, z, c):
    return ((y // 2 * 4 + x) * 2 + c) * 16 + z * 2 + y % 2


def places():
    s = lax.axis_index("space").astype(jnp.uint32)
    b = lax.axis_index("batch").astype(jnp.uint32)
    return (s >> 1) & 3, (s >> 3) * 2 + (b & 1), b >> 1, s & 1


def route(where):
    every = itertools.product(range(4), range(4), range(8), range(2))
    return [(flat(*at), flat(*where(*at))) for at in every]


def swap(block):
    return lax.ppermute(block, BOTH, route(lambda x, y, z, c: (x, y, z, 1 - c)))


def crossed(block, d, swapped):
    def where(x, y, z, c):
        if c == swapped:
            return ((x + d) % 4, y, z, c)
        return (x, (y + d) % 4, z, c)

    return lax.ppermute(block, BOTH, route(where))


def trade_z(blocks):
    groups = [[z * 2 + low_y for z in range(8)] for low_y in range(2)]
    return lax.all_to_all(blocks, "batch", 0, 0, tiled=True, axis_index_groups=groups)


def trade_space(blocks):
    groups = [[chip * 2 + c for chip in range(8)] for c in range(2)]
    return lax.all_to_all(blocks, "space", 0, 0, tiled=True, axis_index_groups=groups)


def at(array, index):
    return lax.dynamic_index_in_dim(array, index, 0, keepdims=False)


def attention_kernel(q_ref, k_ref, v_ref, g_ref, mask_ref, attn_ref, grad_ref):
    full = jnp.float32
    size = 64
    scale = 1.0 / math.sqrt(size)
    over_rows = (((0,), (0,)), ((), ()))
    over_columns = (((1,), (1,)), ((), ()))
    mask = mask_ref[0]
    for head in range(2):
        part = slice(head * size, (head + 1) * size)
        q, k, v, g = q_ref[:, part], k_ref[:, part], v_ref[:, part], g_ref[:, part]
        scores = lax.dot_general(k, q, over_columns, preferred_element_type=full) * scale + mask
        exponent = jnp.exp(scores - jnp.max(scores, 0, keepdims=True))
        probability = exponent * (1.0 / jnp.sum(exponent, 0, keepdims=True))
        low = probability.astype(jnp.bfloat16)
        grad = lax.dot_general(v, g, over_columns, preferred_element_type=full)
        centre = jnp.sum(probability * grad, 0, keepdims=True)
        score_low = (probability * (grad - centre)).astype(jnp.bfloat16)
        attn_ref[:, part] = lax.dot_general(
            low, v, over_rows, preferred_element_type=full
        ).astype(jnp.bfloat16)
        grad_ref[0, :, part] = (
            lax.dot_general(score_low, k, over_rows, preferred_element_type=full) * scale
        ).astype(jnp.bfloat16)
        grad_ref[1, :, part] = (jnp.dot(score_low, q, preferred_element_type=full) * scale).astype(
            jnp.bfloat16
        )
        grad_ref[2, :, part] = jnp.dot(low, g, preferred_element_type=full).astype(jnp.bfloat16)


def attend(qkv, dout, mask):
    rows, width = dout.shape
    pairs = width // 128

    def columns(offset):
        return pl.BlockSpec((ROWS, 128), lambda w, j: (w, offset + j))

    work = 2 * pairs * 2
    return pl.pallas_call(
        attention_kernel,
        grid=(2, pairs),
        in_specs=[
            columns(0),
            columns(pairs),
            columns(2 * pairs),
            columns(0),
            pl.BlockSpec((1, ROWS, ROWS), lambda w, j: (w, 0, 0)),
        ],
        out_specs=[columns(0), pl.BlockSpec((3, ROWS, 128), lambda w, j: (0, w, j))],
        out_shape=[
            jax.ShapeDtypeStruct((rows, width), jnp.bfloat16),
            jax.ShapeDtypeStruct((3, rows, width), jnp.bfloat16),
        ],
        cost_estimate=pl.CostEstimate(
            flops=work * 14 * ROWS * ROWS * 64 * 4,
            bytes_accessed=8 * rows * width * 2,
            transcendentals=work * ROWS * ROWS,
        ),
        compiler_params=pltpu.CompilerParams(vmem_limit_bytes=32 * 2**20),
    )(qkv, qkv, qkv, dout, mask)


LIMIT = pltpu.CompilerParams(vmem_limit_bytes=40 * 2**20)


def cost(flops, bytes_accessed):
    return pl.CostEstimate(flops=flops, bytes_accessed=bytes_accessed, transcendentals=0)


def follow(array, after):
    return pl.pallas_call(
        lambda *refs: None,
        in_specs=[pl.BlockSpec(memory_space=pl.ANY)] * (1 + len(after)),
        out_specs=pl.BlockSpec(memory_space=pl.ANY),
        out_shape=jax.ShapeDtypeStruct(array.shape, array.dtype),
        input_output_aliases={0: 0},
        cost_estimate=cost(0, 0),
    )(array, *after)


def project_kernel(hidden_ref, weight_ref, bias_ref, out_ref):
    out_ref[...] = (
        jnp.dot(hidden_ref[...], weight_ref[0], preferred_element_type=jnp.float32) + bias_ref[...]
    ).astype(jnp.bfloat16)


def project(hidden, weights, biases):
    rows, width = hidden.shape
    return pl.pallas_call(
        project_kernel,
        grid=(6,),
        in_specs=[
            pl.BlockSpec((rows, width), lambda i: (0, 0)),
            pl.BlockSpec((1, width, 256), lambda i: (i, 0, 0)),
            pl.BlockSpec((1, 256), lambda i: (0, i)),
        ],
        out_specs=pl.BlockSpec((rows, 256), lambda i: (0, i)),
        out_shape=jax.ShapeDtypeStruct((rows, 1536), jnp.bfloat16),
        cost_estimate=cost(2 * rows * width * 1536, 8 * 2**20),
        compiler_params=LIMIT,
    )(hidden, weights, biases)


def dout_kernel(grad_ref, kept_ref, got_ref, out_ref):
    total = 0.0
    for i, block in enumerate((kept_ref[0], kept_ref[1], got_ref[0], got_ref[1])):
        total = total + lax.dot_general(
            grad_ref[:, i * 256 : (i + 1) * 256],
            block,
            (((1,), (1,)), ((), ())),
            preferred_element_type=jnp.float32,
        )
    out_ref[...] = total.astype(jnp.bfloat16)


def find_dout(grads, kept, got):
    rows = grads.shape[0]
    return pl.pallas_call(
        dout_kernel,
        out_shape=jax.ShapeDtypeStruct((rows, 512), jnp.bfloat16),
        cost_estimate=cost(2 * rows * 1024 * 512, 4 * 2**20),
        compiler_params=LIMIT,
    )(grads, kept, got)


def terms_kernel(left_ref, right_ref, out_ref):
    out_ref[0] = jnp.dot(left_ref[...], right_ref[0], preferred_element_type=jnp.float32).astype(
        jnp.bfloat16
    )


def find_terms(hidden_t, grad_qkv):
    width, rows = hidden_t.shape
    return pl.pallas_call(
        terms_kernel,
        grid=(6,),
        in_specs=[
            pl.BlockSpec((width, rows), lambda i: (0, 0)),
            pl.BlockSpec((1, rows, 256), lambda i: (i // 2, 0, i % 2)),
        ],
        out_specs=pl.BlockSpec((1, width, 256), lambda i: (i, 0, 0)),
        out_shape=jax.ShapeDtypeStruct((8, width, 256), jnp.bfloat16),
        cost_estimate=cost(2 * rows * width * 1536, 8 * 2**20),
        compiler_params=LIMIT,
    )(hidden_t, grad_qkv)


def last_terms_kernel(left_ref, right_ref, terms_ref, out_ref):
    out_ref[0] = lax.dot_general(
        left_ref[...], right_ref[...], (((0,), (0,)), ((), ())), preferred_element_type=jnp.float32
    ).astype(jnp.bfloat16)


def add_last_terms(attn, grads, terms):
    rows, width = attn.shape
    return pl.pallas_call(
        last_terms_kernel,
        grid=(2,),
        in_specs=[
            pl.BlockSpec((rows, width), lambda i: (0, 0)),
            pl.BlockSpec((rows, 256), lambda i: (0, i)),
            pl.BlockSpec(memory_space=pl.ANY),
        ],
        out_specs=pl.BlockSpec((1, width, 256), lambda i: (6 + i, 0, 0)),
        out_shape=jax.ShapeDtypeStruct(terms.shape, terms.dtype),
        input_output_aliases={2: 0},
        cost_estimate=cost(2 * rows * width * 512, 4 * 2**20),
        compiler_params=LIMIT,
    )(attn, grads, terms)


def hidden_grad_kernel(grad_ref, weight_ref, normed_ref, *rest):
    out_ref, gain_ref, bias_ref = rest[-3:]
    step = pl.program_id(0)
    grad = grad_ref[0]
    bias_ref[0] = jnp.sum(grad.astype(jnp.float32), 0, keepdims=True)
    part = lax.dot_general(
        grad, weight_ref[0], (((1,), (1,)), ((), ())), preferred_element_type=jnp.float32
    )

    @pl.when(step == 0)
    def _():
        out_ref[...] = part

    @pl.when(step > 0)
    def _():
        out_ref[...] += part

    @pl.when(step == 5)
    def _():
        gain_ref[...] = jnp.sum(out_ref[...] * normed_ref[...], 0, keepdims=True)


def find_hidden_grad(grad_qkv, weights, normed, after):
    rows, width = normed.shape
    return pl.pallas_call(
        hidden_grad_kernel,
        grid=(6,),
        in_specs=[
            pl.BlockSpec((1, rows, 256), lambda i: (i // 2, 0, i % 2)),
            pl.BlockSpec((1, width, 256), lambda i: (i, 0, 0)),
            pl.BlockSpec((rows, width), lambda i: (0, 0)),
        ]
        + [pl.BlockSpec(memory_space=pl.ANY)] * len(after),
        out_specs=[
            pl.BlockSpec((rows, width), lambda i: (0, 0)),
            pl.BlockSpec((1, width), lambda i: (0, 0)),
            pl.BlockSpec((1, 1, 256), lambda i: (i, 0, 0)),
        ],
        out_shape=[
            jax.ShapeDtypeStruct((rows, width), jnp.float32),
            jax.ShapeDtypeStruct((1, width), jnp.float32),
            jax.ShapeDtypeStruct((6, 1, 256), jnp.float32),
        ],
        cost_estimate=cost(2 * rows * width * 1536, 14 * 2**20),
        compiler_params=LIMIT,
    )(grad_qkv, weights, normed, *after)


def per_device(inputs, grad_out, fluid, w_qkv, qkv_bias, w_proj, ln_gain):
    full, low = jnp.float32, jnp.bfloat16
    width = w_proj.shape[1]
    half = width // 2
    x, y, z, core = places()
    first = core == 0
    own_rows = w_qkv.shape[0]
    n_space = lax.axis_size("space")
    zero = jnp.uint32(0)

    def block_of(x, y):
        return jnp.where(first, x * 2 + (y >> 1), (y >> 1) * 4 + x)

    def quarter_of(inner):
        return jnp.where(first, (inner & 1) * 2 + (inner >> 1), inner)

    def pairs_of(outer):
        columns = jnp.where(first, outer, outer & 2)
        low_y = jnp.where(first, zero, outer & 1)
        return (columns, low_y), (columns + core, low_y + (1 - core))

    inner_at, outer_at = jnp.where(first, y, x), jnp.where(first, x, y)

    def back(block):
        return lax.ppermute(block, "space", [((i + 1) % n_space, i) for i in range(n_space)])

    walls_plane = jnp.pad(
        fluid[:SHIFT].transpose(1, 2, 0).astype(low), ((0, 0), (0, 0), (0, width - SHIFT))
    )
    rims = back(
        jnp.concatenate([inputs[:, :SHIFT], grad_out[:, :SHIFT], walls_plane[None, None]], 1)
    )
    rim_x, rim_g = rims[:, :SHIFT], rims[:, SHIFT : 2 * SHIFT]
    rim_f = rims[0, 2 * SHIFT, :, :, :SHIFT].transpose(2, 0, 1).astype(fluid.dtype)
    tile_x = jnp.roll(jnp.concatenate([inputs[:, SHIFT:], rim_x], 1), (-SHIFT, -SHIFT), (2, 3))
    tile_g = jnp.roll(jnp.concatenate([grad_out[:, SHIFT:], rim_g], 1), (-SHIFT, -SHIFT), (2, 3))
    tile_f = jnp.roll(jnp.concatenate([fluid[SHIFT:], rim_f], 0), (-SHIFT, -SHIFT), (1, 2))
    extra = ((0, ROWS - TOKENS), (0, 0))
    rows_x = jnp.pad(tile_x.reshape(-1, width), extra)
    rows_g = jnp.pad(tile_g.reshape(-1, width), extra)
    both_x = jnp.concatenate([rows_x, swap(rows_x)], 0).astype(full)
    walls_row = jnp.pad(tile_f.reshape(1, -1).astype(low), ((0, 0), (0, width - TOKENS)))
    padding = jnp.zeros((ROWS - TOKENS - 1, width), low)
    got_g = swap(jnp.concatenate([tile_g.reshape(-1, width), walls_row, padding], 0))
    other_f = got_g[TOKENS, :TOKENS].astype(fluid.dtype)
    grads = jnp.concatenate([rows_g, jnp.pad(got_g[:TOKENS], extra)], 0)
    average = jnp.mean(both_x, -1, keepdims=True)
    centred = both_x - average
    variance = jnp.mean(centred * centred, -1, keepdims=True)
    inv_std = 1.0 / jnp.sqrt(variance + EPS)
    normed = centred * inv_std
    hidden = (normed * ln_gain).astype(low)
    hidden_t = hidden.T
    grads_own_first = jnp.where(
        first, grads, jnp.concatenate([grads[:, half:], grads[:, :half]], 1)
    )

    steps = jnp.arange(WIN, dtype=jnp.int32)
    inner = jnp.where(steps < WIN - SHIFT, 1, 2).astype(jnp.int32)
    last_pair = (x == 3) & (y >= 2)

    def masked(walls, is_last):
        along = jnp.where(is_last, inner, 0)
        labels = along[:, None, None] * 9 + inner[None, :, None] * 3 + inner[None, None, :]
        labels = jnp.pad(labels.reshape(-1), (0, ROWS - TOKENS), constant_values=-1)
        open_keys = jnp.pad(walls.reshape(-1) == 1, (0, ROWS - TOKENS))
        allowed = (labels[:, None] == labels[None, :]) & (
            open_keys[:, None] | jnp.eye(ROWS, dtype=bool)
        )
        return jnp.where(allowed, 0.0, NEG).astype(full)

    mask = jnp.stack([masked(tile_f, last_pair & ~first), masked(other_f, last_pair & first)])

    qkv_parts = w_qkv.reshape(own_rows, 3, 2, half)
    mine = jnp.concatenate(
        [jnp.where(first, qkv_parts[:, i, 0], qkv_parts[:, i, 1]) for i in range(3)]
        + [jnp.where(first, w_proj[:, :half], w_proj[:, half:])],
        1,
    )
    share = lax.dynamic_slice(mine, (zero, block_of(x, y) * 256), (own_rows, 256))
    lined = trade_z(jnp.broadcast_to(share, (8, own_rows, 256)))
    quarters = jnp.zeros((4, 8, own_rows, 256), low)
    for d in range(4):
        piece = crossed(lined, d, 1) if d else lined
        quarters = lax.dynamic_update_slice(
            quarters, piece[None], (quarter_of((inner_at - d) & 3), zero, zero, zero)
        )
    weights = jnp.zeros((4, 2, 8, 2, own_rows, 256), low)
    for d in range(4):
        piece = crossed(quarters, d, 0) if d else quarters
        if d == 1:
            piece = follow(piece, (hidden_t, mask, grads_own_first))
        for i, (columns, low_y) in enumerate(pairs_of((outer_at - d) & 3)):
            weights = lax.dynamic_update_slice(
                weights,
                piece[2 * i : 2 * i + 2].reshape(1, 2, 8, 1, own_rows, 256),
                (columns, zero, zero, low_y, zero, zero),
            )
    weights = weights.reshape(8, width, 256)
    proj = weights[6:]
    kept = lax.dynamic_slice(proj, (zero, core * half, zero), (2, half, 256))
    got = swap(lax.dynamic_slice(proj, (zero, (1 - core) * half, zero), (2, half, 256)))

    biases = qkv_bias.reshape(3, 2, half)
    biases = jnp.where(first, biases[:, 0], biases[:, 1]).reshape(1, -1)
    qkv = project(hidden, weights, biases)
    dout = find_dout(grads_own_first, kept, got)
    attn, grad_qkv = attend(qkv, dout, mask)

    attn_got = swap(attn)
    attn_got = jnp.concatenate([attn_got[ROWS:], attn_got[:ROWS]], 0)
    attn_all = jnp.where(
        first, jnp.concatenate([attn, attn_got], 1), jnp.concatenate([attn_got, attn], 1)
    )
    terms = add_last_terms(attn_all, grads_own_first, find_terms(hidden_t, grad_qkv))
    terms = terms.reshape(4, 2, 8, 2, own_rows, 256)

    def outer_piece(coordinate):
        return jnp.concatenate(
            [
                lax.dynamic_slice(
                    terms, (columns, zero, zero, low_y, zero, zero), (1, 2, 8, 1, own_rows, 256)
                ).reshape(2, 8, own_rows, 256)
                for columns, low_y in pairs_of(coordinate)
            ],
            0,
        )

    pieces = [outer_piece((outer_at + d) & 3) for d in range(4)]
    sums = pieces[0].astype(full)
    for d in range(1, 4):
        sums = sums + crossed(pieces[d], d, 0).astype(full)
    sums = sums.astype(low)

    partial, gain_term, bias_term = find_hidden_grad(grad_qkv, weights, normed, pieces[1:])
    bias_term = bias_term.reshape(3, 1, half)
    nothing = jnp.zeros_like(bias_term)
    bias_term = jnp.where(
        first,
        jnp.concatenate([bias_term, nothing], 1),
        jnp.concatenate([nothing, bias_term], 1),
    )
    small = jnp.concatenate([gain_term.reshape(-1), bias_term.reshape(-1)]).reshape(16, 256)
    small = small + swap(small)

    def split(values):
        upper = lax.reduce_precision(values, 8, 7)
        return jnp.concatenate([upper.astype(low), (values - upper).astype(low)], 0)

    def joined(rows):
        return rows[-32:-16].astype(full) + rows[-16:].astype(full)

    def with_small(rows, extra_rows):
        return jnp.concatenate([rows.reshape(-1, 256), extra_rows], 0)

    extra_rows = split(small)
    total = at(sums, quarter_of(inner_at)).reshape(-1, 256).astype(full)
    for d in range(1, 4):
        piece = at(sums, quarter_of((inner_at + d) & 3))
        arrived = crossed(with_small(piece, extra_rows), d, 1)
        total = total + arrived[:-32].astype(full)
        small = small + joined(arrived)
    sums = total.astype(low).reshape(8, own_rows, 256)
    repeated = jnp.broadcast_to(split(small), (8, 32, 256))
    arrived = trade_z(jnp.concatenate([sums, repeated], 1))
    small = jnp.sum(arrived[:, own_rows:].astype(full), 0)
    small = small[:16] + small[16:]
    final = with_small(
        jnp.sum(arrived[:, :own_rows].astype(full), 0).astype(low), split(small)
    )
    arrived = trade_space(jnp.broadcast_to(final, (8, own_rows + 32, 256)))
    small = jnp.sum(arrived[:4, own_rows:].astype(full), 0)
    small = small[:16] + small[16:]
    rows = arrived[:, :own_rows]
    rows = jnp.where(
        first, rows.reshape(2, 4, own_rows, 256).swapaxes(0, 1).reshape(rows.shape), rows
    )
    others = swap(rows)
    small_got = swap(small)
    small = jnp.where(first, small, small_got).reshape(-1)
    sides = (jnp.where(first, rows, others), jnp.where(first, others, rows))
    blocks = [side[2 * i + j].astype(full) for i in range(4) for side in sides for j in range(2)]
    out_qkv = jnp.concatenate(blocks[:12], 1)
    out_proj = jnp.concatenate(blocks[12:], 1)

    grad_hidden = partial[:ROWS] + swap(partial[ROWS:])
    grad_norm = grad_hidden * ln_gain
    own_normed = normed[:ROWS]
    grad_flat = rows_g.astype(full) + inv_std[:ROWS] * (
        grad_norm
        - jnp.mean(grad_norm, -1, keepdims=True)
        - own_normed * jnp.mean(grad_norm * own_normed, -1, keepdims=True)
    )
    grad_tile = jnp.roll(
        grad_flat[:TOKENS].astype(low).reshape(tile_x.shape), (SHIFT, SHIFT), (2, 3)
    )
    returned = lax.ppermute(
        grad_tile[:, WIN - SHIFT :], "space", [(i, (i + 1) % n_space) for i in range(n_space)]
    )
    grad_input = jnp.concatenate([returned, grad_tile[:, : WIN - SHIFT]], 1)
    return (grad_input, out_qkv, out_proj, small[:width], small[width:])


def solution(mesh):
    tokens = P("batch", "space", None, None, None)
    return jax.shard_map(
        per_device,
        mesh=mesh,
        in_specs=(tokens, tokens, P("space", None, None), P("batch", None), P(), P("batch", None), P()),
        out_specs=(tokens, P("batch", None), P("batch", None), P(), P()),
        check_vma=False,
    )
```

```python
import itertools
import math

import jax
import jax.numpy as jnp
from jax import lax
from jax.experimental import pallas as pl
from jax.experimental.pallas import tpu as pltpu
from jax.sharding import PartitionSpec as P

HEADS = 16
WIN = 7
SHIFT = 3
TOKENS = WIN**3
ROWS = 352
EPS = 1e-05
NEG = -1e30
BOTH = ("space", "batch")


def flat(x, y, z, c):
    return ((y // 2 * 4 + x) * 2 + c) * 16 + z * 2 + y % 2


def places():
    s = lax.axis_index("space").astype(jnp.uint32)
    b = lax.axis_index("batch").astype(jnp.uint32)
    return (s >> 1) & 3, (s >> 3) * 2 + (b & 1), b >> 1, s & 1


def route(where):
    every = itertools.product(range(4), range(4), range(8), range(2))
    return [(flat(*at), flat(*where(*at))) for at in every]


def swap(block):
    return lax.ppermute(block, BOTH, route(lambda x, y, z, c: (x, y, z, 1 - c)))


def crossed(block, d, swapped):
    def where(x, y, z, c):
        if c == swapped:
            return ((x + d) % 4, y, z, c)
        return (x, (y + d) % 4, z, c)

    return lax.ppermute(block, BOTH, route(where))


def trade_z(blocks):
    groups = [[z * 2 + low_y for z in range(8)] for low_y in range(2)]
    return lax.all_to_all(blocks, "batch", 0, 0, tiled=True, axis_index_groups=groups)


def trade_space(blocks):
    groups = [[chip * 2 + c for chip in range(8)] for c in range(2)]
    return lax.all_to_all(blocks, "space", 0, 0, tiled=True, axis_index_groups=groups)


def at(array, index):
    return lax.dynamic_index_in_dim(array, index, 0, keepdims=False)


def attention_kernel(q_ref, k_ref, v_ref, g_ref, mask_ref, attn_ref, grad_ref):
    full = jnp.float32
    size = 64
    scale = 1.0 / math.sqrt(size)
    over_rows = (((0,), (0,)), ((), ()))
    over_columns = (((1,), (1,)), ((), ()))
    mask = mask_ref[0]
    for_queries = []
    for head in range(2):
        part = slice(head * size, (head + 1) * size)
        q, k, v, g = q_ref[:, part], k_ref[:, part], v_ref[:, part], g_ref[:, part]
        scaled = q * jnp.bfloat16(scale)
        scores = lax.dot_general(k, scaled, over_columns, preferred_element_type=full) + mask
        exponent = jnp.exp(scores - jnp.max(scores, 0, keepdims=True))
        probability = exponent * (1.0 / jnp.sum(exponent, 0, keepdims=True))
        low = probability.astype(jnp.bfloat16)
        grad = lax.dot_general(v, g, over_columns, preferred_element_type=full)
        centre = jnp.sum(probability * grad, 0, keepdims=True)
        score_low = (probability * (grad - centre)).astype(jnp.bfloat16)
        attn_t = lax.dot_general(v, low, over_rows, preferred_element_type=full)
        grad_q_t = lax.dot_general(k, score_low, over_rows, preferred_element_type=full) * scale
        for_queries.append((attn_t.astype(jnp.bfloat16), grad_q_t.astype(jnp.bfloat16)))
        grad_ref[1, :, part] = (
            jnp.dot(score_low, q, preferred_element_type=full) * scale
        ).astype(jnp.bfloat16)
        grad_ref[2, :, part] = jnp.dot(low, g, preferred_element_type=full).astype(jnp.bfloat16)
    attn_ref[...] = jnp.concatenate([attn for attn, _ in for_queries], 0).T
    grad_ref[0] = jnp.concatenate([grad for _, grad in for_queries], 0).T


def attend(qkv, dout, mask):
    rows, width = dout.shape
    pairs = width // 128

    def columns(offset):
        return pl.BlockSpec((ROWS, 128), lambda w, j: (w, offset + j))

    work = 2 * pairs * 2
    return pl.pallas_call(
        attention_kernel,
        grid=(2, pairs),
        in_specs=[
            columns(0),
            columns(pairs),
            columns(2 * pairs),
            columns(0),
            pl.BlockSpec((1, ROWS, ROWS), lambda w, j: (w, 0, 0)),
        ],
        out_specs=[columns(0), pl.BlockSpec((3, ROWS, 128), lambda w, j: (0, w, j))],
        out_shape=[
            jax.ShapeDtypeStruct((rows, width), jnp.bfloat16),
            jax.ShapeDtypeStruct((3, rows, width), jnp.bfloat16),
        ],
        cost_estimate=pl.CostEstimate(
            flops=work * 14 * ROWS * ROWS * 64 * 4,
            bytes_accessed=8 * rows * width * 2,
            transcendentals=work * ROWS * ROWS,
        ),
        compiler_params=pltpu.CompilerParams(vmem_limit_bytes=58 * 2**20),
    )(qkv, qkv, qkv, dout, mask)


LIMIT = pltpu.CompilerParams(vmem_limit_bytes=58 * 2**20)


def cost(flops, bytes_accessed):
    return pl.CostEstimate(flops=flops, bytes_accessed=bytes_accessed, transcendentals=0)


def follow(array, after):
    return pl.pallas_call(
        lambda *refs: None,
        in_specs=[pl.BlockSpec(memory_space=pl.ANY)] * (1 + len(after)),
        out_specs=pl.BlockSpec(memory_space=pl.ANY),
        out_shape=jax.ShapeDtypeStruct(array.shape, array.dtype),
        input_output_aliases={0: 0},
        cost_estimate=cost(0, 0),
    )(array, *after)


def project_kernel(hidden_ref, weight_ref, bias_ref, out_ref):
    out_ref[...] = (
        jnp.dot(hidden_ref[...], weight_ref[0], preferred_element_type=jnp.float32) + bias_ref[...]
    ).astype(jnp.bfloat16)


def project(hidden, weights, biases):
    rows, width = hidden.shape
    return pl.pallas_call(
        project_kernel,
        grid=(6,),
        in_specs=[
            pl.BlockSpec((rows, width), lambda i: (0, 0)),
            pl.BlockSpec((1, width, 256), lambda i: (i, 0, 0)),
            pl.BlockSpec((1, 256), lambda i: (0, i)),
        ],
        out_specs=pl.BlockSpec((rows, 256), lambda i: (0, i)),
        out_shape=jax.ShapeDtypeStruct((rows, 1536), jnp.bfloat16),
        cost_estimate=cost(2 * rows * width * 1536, 8 * 2**20),
        compiler_params=LIMIT,
    )(hidden, weights, biases)


def dout_kernel(grad_ref, kept_ref, got_ref, out_ref):
    total = 0.0
    for i, block in enumerate((kept_ref[0], kept_ref[1], got_ref[0], got_ref[1])):
        total = total + lax.dot_general(
            grad_ref[:, i * 256 : (i + 1) * 256],
            block,
            (((1,), (1,)), ((), ())),
            preferred_element_type=jnp.float32,
        )
    out_ref[...] = total.astype(jnp.bfloat16)


def find_dout(grads, kept, got):
    rows = grads.shape[0]
    return pl.pallas_call(
        dout_kernel,
        out_shape=jax.ShapeDtypeStruct((rows, 512), jnp.bfloat16),
        cost_estimate=cost(2 * rows * 1024 * 512, 4 * 2**20),
        compiler_params=LIMIT,
    )(grads, kept, got)


def terms_kernel(left_ref, right_ref, out_ref):
    out_ref[0] = jnp.dot(left_ref[...], right_ref[0], preferred_element_type=jnp.float32).astype(
        jnp.bfloat16
    )


def find_terms(hidden_t, grad_qkv):
    width, rows = hidden_t.shape
    return pl.pallas_call(
        terms_kernel,
        grid=(6,),
        in_specs=[
            pl.BlockSpec((width, rows), lambda i: (0, 0)),
            pl.BlockSpec((1, rows, 256), lambda i: (i // 2, 0, i % 2)),
        ],
        out_specs=pl.BlockSpec((1, width, 256), lambda i: (i, 0, 0)),
        out_shape=jax.ShapeDtypeStruct((8, width, 256), jnp.bfloat16),
        cost_estimate=cost(2 * rows * width * 1536, 8 * 2**20),
        compiler_params=LIMIT,
    )(hidden_t, grad_qkv)


def last_terms_kernel(left_ref, right_ref, terms_ref, out_ref):
    out_ref[0] = lax.dot_general(
        left_ref[...], right_ref[...], (((0,), (0,)), ((), ())), preferred_element_type=jnp.float32
    ).astype(jnp.bfloat16)


def add_last_terms(attn, grads, terms):
    rows, width = attn.shape
    return pl.pallas_call(
        last_terms_kernel,
        grid=(2,),
        in_specs=[
            pl.BlockSpec((rows, width), lambda i: (0, 0)),
            pl.BlockSpec((rows, 256), lambda i: (0, i)),
            pl.BlockSpec(memory_space=pl.ANY),
        ],
        out_specs=pl.BlockSpec((1, width, 256), lambda i: (6 + i, 0, 0)),
        out_shape=jax.ShapeDtypeStruct(terms.shape, terms.dtype),
        input_output_aliases={2: 0},
        cost_estimate=cost(2 * rows * width * 512, 4 * 2**20),
        compiler_params=LIMIT,
    )(attn, grads, terms)


def hidden_grad_kernel(grad_ref, weight_ref, normed_ref, *rest):
    out_ref, gain_ref, bias_ref = rest[-3:]
    step = pl.program_id(0)
    grad = grad_ref[0]
    bias_ref[0] = jnp.sum(grad.astype(jnp.float32), 0, keepdims=True)
    part = lax.dot_general(
        grad, weight_ref[0], (((1,), (1,)), ((), ())), preferred_element_type=jnp.float32
    )

    @pl.when(step == 0)
    def _():
        out_ref[...] = part

    @pl.when(step > 0)
    def _():
        out_ref[...] += part

    @pl.when(step == 5)
    def _():
        gain_ref[...] = jnp.sum(out_ref[...] * normed_ref[...], 0, keepdims=True)


def find_hidden_grad(grad_qkv, weights, normed, after):
    rows, width = normed.shape
    return pl.pallas_call(
        hidden_grad_kernel,
        grid=(6,),
        in_specs=[
            pl.BlockSpec((1, rows, 256), lambda i: (i // 2, 0, i % 2)),
            pl.BlockSpec((1, width, 256), lambda i: (i, 0, 0)),
            pl.BlockSpec((rows, width), lambda i: (0, 0)),
        ]
        + [pl.BlockSpec(memory_space=pl.ANY)] * len(after),
        out_specs=[
            pl.BlockSpec((rows, width), lambda i: (0, 0)),
            pl.BlockSpec((1, width), lambda i: (0, 0)),
            pl.BlockSpec((1, 1, 256), lambda i: (i, 0, 0)),
        ],
        out_shape=[
            jax.ShapeDtypeStruct((rows, width), jnp.float32),
            jax.ShapeDtypeStruct((1, width), jnp.float32),
            jax.ShapeDtypeStruct((6, 1, 256), jnp.float32),
        ],
        cost_estimate=cost(2 * rows * width * 1536, 14 * 2**20),
        compiler_params=LIMIT,
    )(grad_qkv, weights, normed, *after)


def per_device(inputs, grad_out, fluid, w_qkv, qkv_bias, w_proj, ln_gain):
    full, low = jnp.float32, jnp.bfloat16
    width = w_proj.shape[1]
    half = width // 2
    x, y, z, core = places()
    first = core == 0
    own_rows = w_qkv.shape[0]
    n_space = lax.axis_size("space")
    zero = jnp.uint32(0)

    def block_of(x, y):
        return jnp.where(first, x * 2 + (y >> 1), (y >> 1) * 4 + x)

    def quarter_of(inner):
        return jnp.where(first, (inner & 1) * 2 + (inner >> 1), inner)

    def pairs_of(outer):
        columns = jnp.where(first, outer, outer & 2)
        low_y = jnp.where(first, zero, outer & 1)
        return (columns, low_y), (columns + core, low_y + (1 - core))

    def unit_of(outer, inner):
        return (
            jnp.where(first, outer, (outer & 2) + (inner >> 1)),
            jnp.where(first, inner >> 1, inner & 1),
            jnp.where(first, inner, outer) & 1,
        )

    inner_at, outer_at = jnp.where(first, y, x), jnp.where(first, x, y)

    def back(block):
        return lax.ppermute(block, "space", [((i + 1) % n_space, i) for i in range(n_space)])

    walls_plane = jnp.pad(
        fluid[:SHIFT].transpose(1, 2, 0).astype(low), ((0, 0), (0, 0), (0, width - SHIFT))
    )
    rims = back(
        jnp.concatenate([inputs[:, :SHIFT], grad_out[:, :SHIFT], walls_plane[None, None]], 1)
    )
    rim_x, rim_g = rims[:, :SHIFT], rims[:, SHIFT : 2 * SHIFT]
    rim_f = rims[0, 2 * SHIFT, :, :, :SHIFT].transpose(2, 0, 1).astype(fluid.dtype)
    tile_x = jnp.roll(jnp.concatenate([inputs[:, SHIFT:], rim_x], 1), (-SHIFT, -SHIFT), (2, 3))
    tile_g = jnp.roll(jnp.concatenate([grad_out[:, SHIFT:], rim_g], 1), (-SHIFT, -SHIFT), (2, 3))
    tile_f = jnp.roll(jnp.concatenate([fluid[SHIFT:], rim_f], 0), (-SHIFT, -SHIFT), (1, 2))
    extra = ((0, ROWS - TOKENS), (0, 0))
    rows_x = jnp.pad(tile_x.reshape(-1, width), extra)
    rows_g = jnp.pad(tile_g.reshape(-1, width), extra)
    both_x = jnp.concatenate([rows_x, swap(rows_x)], 0).astype(full)
    walls_row = jnp.pad(tile_f.reshape(1, -1).astype(low), ((0, 0), (0, width - TOKENS)))
    padding = jnp.zeros((ROWS - TOKENS - 1, width), low)
    got_g = swap(jnp.concatenate([tile_g.reshape(-1, width), walls_row, padding], 0))
    other_f = got_g[TOKENS, :TOKENS].astype(fluid.dtype)
    grads = jnp.concatenate([rows_g, jnp.pad(got_g[:TOKENS], extra)], 0)
    average = jnp.mean(both_x, -1, keepdims=True)
    centred = both_x - average
    variance = jnp.mean(centred * centred, -1, keepdims=True)
    inv_std = 1.0 / jnp.sqrt(variance + EPS)
    normed = centred * inv_std
    hidden = (normed * ln_gain).astype(low)
    hidden_t = hidden.T
    grads_own_first = jnp.where(
        first, grads, jnp.concatenate([grads[:, half:], grads[:, :half]], 1)
    )

    steps = jnp.arange(WIN, dtype=jnp.int32)
    inner = jnp.where(steps < WIN - SHIFT, 1, 2).astype(jnp.int32)
    last_pair = (x == 3) & (y >= 2)

    def masked(walls, is_last):
        along = jnp.where(is_last, inner, 0)
        labels = along[:, None, None] * 9 + inner[None, :, None] * 3 + inner[None, None, :]
        labels = jnp.pad(labels.reshape(-1), (0, ROWS - TOKENS), constant_values=-1)
        open_keys = jnp.pad(walls.reshape(-1) == 1, (0, ROWS - TOKENS))
        allowed = (labels[:, None] == labels[None, :]) & (
            open_keys[:, None] | jnp.eye(ROWS, dtype=bool)
        )
        return jnp.where(allowed, 0.0, NEG).astype(full)

    mask = jnp.stack([masked(tile_f, last_pair & ~first), masked(other_f, last_pair & first)])

    qkv_parts = w_qkv.reshape(own_rows, 3, 2, half)
    mine = jnp.concatenate(
        [jnp.where(first, qkv_parts[:, i, 0], qkv_parts[:, i, 1]) for i in range(3)]
        + [jnp.where(first, w_proj[:, :half], w_proj[:, half:])],
        1,
    )
    share = lax.dynamic_slice(mine, (zero, block_of(x, y) * 256), (own_rows, 256))
    lined = trade_z(jnp.broadcast_to(share, (8, own_rows, 256)))
    quarters = jnp.stack([lined] + [crossed(lined, d, 1) for d in range(1, 4)])
    weights = jnp.zeros((4, 2, 8, 2, own_rows, 256), low)
    for d in range(4):
        piece = crossed(quarters, d, 0) if d else quarters
        if d == 1:
            piece = follow(piece, (hidden_t, mask, grads_own_first))
        for e in range(4):
            columns, side, low_y = unit_of((outer_at - d) & 3, (inner_at - e) & 3)
            weights = lax.dynamic_update_slice(
                weights,
                piece[e].reshape(1, 1, 8, 1, own_rows, 256),
                (columns, side, zero, low_y, zero, zero),
            )
    weights = weights.reshape(8, width, 256)
    six = jnp.uint32(6)
    kept = lax.dynamic_slice(weights, (six, core * half, zero), (2, half, 256))
    got = swap(lax.dynamic_slice(weights, (six, (1 - core) * half, zero), (2, half, 256)))

    biases = qkv_bias.reshape(3, 2, half)
    biases = jnp.where(first, biases[:, 0], biases[:, 1]).reshape(1, -1)
    qkv = project(hidden, weights, biases)
    dout = find_dout(grads_own_first, kept, got)
    attn, grad_qkv = attend(qkv, dout, mask)

    attn_got = swap(attn)
    attn_got = jnp.concatenate([attn_got[ROWS:], attn_got[:ROWS]], 0)
    attn_all = jnp.where(
        first, jnp.concatenate([attn, attn_got], 1), jnp.concatenate([attn_got, attn], 1)
    )
    terms = add_last_terms(attn_all, grads_own_first, find_terms(hidden_t, grad_qkv))
    terms = terms.reshape(4, 2, 8, 2, own_rows, 256)

    def outer_piece(coordinate):
        return jnp.concatenate(
            [
                lax.dynamic_slice(
                    terms, (columns, zero, zero, low_y, zero, zero), (1, 2, 8, 1, own_rows, 256)
                ).reshape(2, 8, own_rows, 256)
                for columns, low_y in pairs_of(coordinate)
            ],
            0,
        )

    pieces = [outer_piece((outer_at + d) & 3) for d in range(4)]
    sums = pieces[0].astype(full)
    for d in range(1, 4):
        sums = sums + crossed(pieces[d], d, 0).astype(full)
    sums = sums.astype(low)

    partial, gain_term, bias_term = find_hidden_grad(grad_qkv, weights, normed, [piece[0, 0, :16, :128] for piece in pieces[1:]])
    bias_term = bias_term.reshape(3, 1, half)
    nothing = jnp.zeros_like(bias_term)
    bias_term = jnp.where(
        first,
        jnp.concatenate([bias_term, nothing], 1),
        jnp.concatenate([nothing, bias_term], 1),
    )
    small = jnp.concatenate([gain_term.reshape(-1), bias_term.reshape(-1)]).reshape(16, 256)
    small = small + swap(small)

    def split(values):
        upper = lax.reduce_precision(values, 8, 7)
        return jnp.concatenate([upper.astype(low), (values - upper).astype(low)], 0)

    def joined(rows):
        return rows[-32:-16].astype(full) + rows[-16:].astype(full)

    def with_small(rows, extra_rows):
        return jnp.concatenate([rows.reshape(-1, 256), extra_rows], 0)

    extra_rows = split(small)
    total = at(sums, quarter_of(inner_at)).reshape(-1, 256).astype(full)
    for d in range(1, 4):
        piece = at(sums, quarter_of((inner_at + d) & 3))
        arrived = crossed(with_small(piece, extra_rows), d, 1)
        total = total + arrived[:-32].astype(full)
        small = small + joined(arrived)
    sums = total.astype(low).reshape(8, own_rows, 256)
    repeated = jnp.broadcast_to(small.astype(low), (8, 16, 256))
    arrived = trade_z(jnp.concatenate([sums, repeated], 1))
    final = jnp.sum(arrived.astype(full), 0).astype(low)
    arrived = trade_space(jnp.broadcast_to(final, (8, own_rows + 16, 256)))
    small = jnp.sum(arrived[:4, own_rows:].astype(full), 0)
    rows = arrived[:, :own_rows]
    rows = jnp.where(
        first, rows.reshape(2, 4, own_rows, 256).swapaxes(0, 1).reshape(rows.shape), rows
    )
    others = swap(rows)
    small_got = swap(small)
    small = jnp.where(first, small, small_got).reshape(-1)
    sides = (jnp.where(first, rows, others), jnp.where(first, others, rows))
    blocks = [side[2 * i + j].astype(full) for i in range(4) for side in sides for j in range(2)]
    out_qkv = jnp.concatenate(blocks[:12], 1)
    out_proj = jnp.concatenate(blocks[12:], 1)

    grad_hidden = partial[:ROWS] + swap(partial[ROWS:])
    grad_norm = grad_hidden * ln_gain
    own_normed = normed[:ROWS]
    grad_flat = rows_g.astype(full) + inv_std[:ROWS] * (
        grad_norm
        - jnp.mean(grad_norm, -1, keepdims=True)
        - own_normed * jnp.mean(grad_norm * own_normed, -1, keepdims=True)
    )
    grad_tile = jnp.roll(
        grad_flat[:TOKENS].astype(low).reshape(tile_x.shape), (SHIFT, SHIFT), (2, 3)
    )
    returned = lax.ppermute(
        grad_tile[:, WIN - SHIFT :], "space", [(i, (i + 1) % n_space) for i in range(n_space)]
    )
    grad_input = jnp.concatenate([returned, grad_tile[:, : WIN - SHIFT]], 1)
    return (grad_input, out_qkv, out_proj, small[:width], small[width:])


def solution(mesh):
    tokens = P("batch", "space", None, None, None)
    return jax.shard_map(
        per_device,
        mesh=mesh,
        in_specs=(tokens, tokens, P("space", None, None), P("batch", None), P(), P("batch", None), P()),
        out_specs=(tokens, P("batch", None), P("batch", None), P(), P()),
        check_vma=False,
    )
```

```python
import itertools
import math

import jax
import jax.numpy as jnp
from jax import lax
from jax.experimental import pallas as pl
from jax.experimental.pallas import tpu as pltpu
from jax.sharding import PartitionSpec as P

HEADS = 16
WIN = 7
SHIFT = 3
TOKENS = WIN**3
ROWS = 352
EPS = 1e-05
NEG = -1e30
BOTH = ("space", "batch")


def flat(x, y, z, c):
    return ((y // 2 * 4 + x) * 2 + c) * 16 + z * 2 + y % 2


def places():
    s = lax.axis_index("space").astype(jnp.uint32)
    b = lax.axis_index("batch").astype(jnp.uint32)
    return (s >> 1) & 3, (s >> 3) * 2 + (b & 1), b >> 1, s & 1


def route(where):
    every = itertools.product(range(4), range(4), range(8), range(2))
    return [(flat(*at), flat(*where(*at))) for at in every]


def swap(block):
    return lax.ppermute(block, BOTH, route(lambda x, y, z, c: (x, y, z, 1 - c)))


def crossed(block, d, swapped):
    def where(x, y, z, c):
        if c == swapped:
            return ((x + d) % 4, y, z, c)
        return (x, (y + d) % 4, z, c)

    return lax.ppermute(block, BOTH, route(where))


def trade_z(blocks):
    groups = [[z * 2 + low_y for z in range(8)] for low_y in range(2)]
    return lax.all_to_all(blocks, "batch", 0, 0, tiled=True, axis_index_groups=groups)


def trade_space(blocks):
    groups = [[chip * 2 + c for chip in range(8)] for c in range(2)]
    return lax.all_to_all(blocks, "space", 0, 0, tiled=True, axis_index_groups=groups)


def attention_kernel(q_ref, k_ref, v_ref, g_ref, mask_ref, attn_ref, grad_ref):
    full = jnp.float32
    size = 64
    scale = 1.0 / math.sqrt(size)
    over_rows = (((0,), (0,)), ((), ()))
    over_columns = (((1,), (1,)), ((), ()))
    mask = mask_ref[0]
    for_queries = []
    for head in range(4):
        part = slice(head * size, (head + 1) * size)
        q, k, v, g = q_ref[:, part], k_ref[:, part], v_ref[:, part], g_ref[:, part]
        scaled = q * jnp.bfloat16(scale)
        scores = lax.dot_general(k, scaled, over_columns, preferred_element_type=full) + mask
        exponent = jnp.exp(scores - jnp.max(scores, 0, keepdims=True))
        probability = exponent * (1.0 / jnp.sum(exponent, 0, keepdims=True))
        low = probability.astype(jnp.bfloat16)
        grad = lax.dot_general(v, g, over_columns, preferred_element_type=full)
        centre = jnp.sum(probability * grad, 0, keepdims=True)
        score_low = (probability * (grad - centre)).astype(jnp.bfloat16)
        attn_t = lax.dot_general(v, low, over_rows, preferred_element_type=full)
        grad_q_t = lax.dot_general(k, score_low, over_rows, preferred_element_type=full) * scale
        for_queries.append((attn_t.astype(jnp.bfloat16), grad_q_t.astype(jnp.bfloat16)))
        grad_ref[1, :, part] = (
            jnp.dot(score_low, q, preferred_element_type=full) * scale
        ).astype(jnp.bfloat16)
        grad_ref[2, :, part] = jnp.dot(low, g, preferred_element_type=full).astype(jnp.bfloat16)
    for parity in range(2):
        attn_ref[parity] = jnp.concatenate(
            [attn for attn, _ in for_queries[parity::2]], 0
        ).T
    grad_ref[0] = jnp.concatenate([grad for _, grad in for_queries], 0).T


def attend(qkv, dout, mask):
    rows, width = dout.shape
    groups = width // 256

    def columns(offset):
        return pl.BlockSpec((ROWS, 256), lambda w, j: (w, offset + j))

    work = 2 * groups * 4
    return pl.pallas_call(
        attention_kernel,
        grid=(2, groups),
        in_specs=[
            columns(0),
            columns(groups),
            columns(2 * groups),
            columns(0),
            pl.BlockSpec((1, ROWS, ROWS), lambda w, j: (w, 0, 0)),
        ],
        out_specs=[
            pl.BlockSpec((2, ROWS, 128), lambda w, j: (0, w, j)),
            pl.BlockSpec((3, ROWS, 256), lambda w, j: (0, w, j)),
        ],
        out_shape=[
            jax.ShapeDtypeStruct((2, rows, width // 2), jnp.bfloat16),
            jax.ShapeDtypeStruct((3, rows, width), jnp.bfloat16),
        ],
        cost_estimate=pl.CostEstimate(
            flops=work * 14 * ROWS * ROWS * 64 * 4,
            bytes_accessed=8 * rows * width * 2,
            transcendentals=work * ROWS * ROWS,
        ),
        compiler_params=pltpu.CompilerParams(vmem_limit_bytes=24 * 2**20),
    )(qkv, qkv, qkv, dout, mask)


SMALL = pltpu.CompilerParams(vmem_limit_bytes=2**20)
LIMIT = pltpu.CompilerParams(vmem_limit_bytes=20 * 2**20)
LARGE = pltpu.CompilerParams(vmem_limit_bytes=30 * 2**20)


def cost(flops, bytes_accessed):
    return pl.CostEstimate(flops=flops, bytes_accessed=bytes_accessed, transcendentals=0)


def follow(array, after):
    return pl.pallas_call(
        lambda *refs: None,
        in_specs=[pl.BlockSpec(memory_space=pl.ANY)] * (1 + len(after)),
        out_specs=pl.BlockSpec(memory_space=pl.ANY),
        out_shape=jax.ShapeDtypeStruct(array.shape, array.dtype),
        input_output_aliases={0: 0},
        cost_estimate=cost(0, 0),
        compiler_params=SMALL,
    )(array, *after)


SMEM = pl.BlockSpec(memory_space=pltpu.SMEM)
VMEM = pl.BlockSpec(memory_space=pltpu.VMEM)


def each_unit(table_ref, weights, visit):
    for d, ref in enumerate(weights):

        @pl.loop(0, 4)
        def _(e):
            visit(table_ref[d * 4 + e], table_ref[16 + d * 4 + e], ref.at[e])


def pick_kernel(table_ref, w0, w1, w2, w3, kept_ref, sent_ref):
    core = table_ref[32]

    def visit(block, low_y, ref):
        @pl.when(block >= 6)
        def _():
            spot = low_y * 2 + block - 6
            kept_ref[spot] = ref[pl.ds(pl.multiple_of(core * 256, 256), 256), :]
            sent_ref[spot] = ref[pl.ds(pl.multiple_of((1 - core) * 256, 256), 256), :]

    each_unit(table_ref, (w0, w1, w2, w3), visit)


def pick(table, weights):
    return pl.pallas_call(
        pick_kernel,
        in_specs=[SMEM] + [VMEM] * 4,
        out_specs=[VMEM] * 2,
        out_shape=[jax.ShapeDtypeStruct((4, 256, 256), jnp.bfloat16)] * 2,
        cost_estimate=cost(0, 5 * 2**20),
        compiler_params=LIMIT,
    )(table, *weights)


def project_kernel(table_ref, hidden_ref, w0, w1, w2, w3, bias_ref, out_ref, total_ref):
    for block in range(6):
        total_ref[block] = jnp.broadcast_to(bias_ref[block], total_ref.shape[1:])

    def visit(block, low_y, ref):
        @pl.when(block < 6)
        def _():
            total_ref[block] += jnp.dot(
                hidden_ref[low_y], ref[...], preferred_element_type=jnp.float32
            )

    each_unit(table_ref, (w0, w1, w2, w3), visit)
    for block in range(6):
        out_ref[:, block * 256 : (block + 1) * 256] = total_ref[block].astype(jnp.bfloat16)


def project(table, hidden, weights, biases):
    rows = hidden.shape[1]
    return pl.pallas_call(
        project_kernel,
        in_specs=[SMEM] + [VMEM] * 6,
        out_specs=VMEM,
        out_shape=jax.ShapeDtypeStruct((rows, 1536), jnp.bfloat16),
        scratch_shapes=[pltpu.VMEM((6, rows, 256), jnp.float32)],
        cost_estimate=cost(2 * rows * 1024 * 1536, 8 * 2**20),
        compiler_params=LIMIT,
    )(table, hidden, *weights, biases)


def dout_kernel(grad_ref, kept_ref, got_ref, out_ref):
    for low_y in range(2):
        total = 0.0
        for i in range(4):
            ref = kept_ref if i < 2 else got_ref
            total = total + lax.dot_general(
                grad_ref[:, i * 256 : (i + 1) * 256],
                ref[low_y * 2 + i % 2],
                (((1,), (1,)), ((), ())),
                preferred_element_type=jnp.float32,
            )
        total = total.astype(jnp.bfloat16)
        for i in range(4):
            head = 2 * i + low_y
            out_ref[:, head * 64 : (head + 1) * 64] = total[:, i * 64 : (i + 1) * 64]


def find_dout(grads, kept, got):
    rows = grads.shape[0]
    return pl.pallas_call(
        dout_kernel,
        in_specs=[VMEM] * 3,
        out_specs=VMEM,
        out_shape=jax.ShapeDtypeStruct((rows, 512), jnp.bfloat16),
        cost_estimate=cost(2 * rows * 1024 * 512, 4 * 2**20),
        compiler_params=LIMIT,
    )(grads, kept, got)


def terms_kernel(spots_ref, left_ref, right_ref, out_ref):
    out_ref[0] = jnp.dot(
        left_ref[0], right_ref[0], preferred_element_type=jnp.float32
    ).astype(jnp.bfloat16)


def find_terms(spots, hidden_t, grad_qkv):
    _, half, rows = hidden_t.shape
    return pl.pallas_call(
        terms_kernel,
        grid_spec=pltpu.PrefetchScalarGridSpec(
            num_scalar_prefetch=1,
            grid=(12,),
            in_specs=[
                pl.BlockSpec((1, half, rows), lambda i, spots: (i // 6, 0, 0)),
                pl.BlockSpec((1, rows, 256), lambda i, spots: (i % 6 // 2, 0, i % 2)),
            ],
            out_specs=pl.BlockSpec((1, half, 256), lambda i, spots: (spots[i], 0, 0)),
        ),
        out_shape=jax.ShapeDtypeStruct((16, half, 256), jnp.bfloat16),
        cost_estimate=cost(2 * rows * half * 3072, 8 * 2**20),
        compiler_params=LIMIT,
    )(spots, hidden_t, grad_qkv)


def last_terms_kernel(spots_ref, attn_ref, got_ref, grads_ref, terms_ref, out_ref):
    core = spots_ref[16]
    rows = grads_ref.shape[0] // 2
    grads = grads_ref[...]

    def product(left, right):
        return lax.dot_general(
            left, right, (((0,), (0,)), ((), ())), preferred_element_type=jnp.float32
        )

    out_ref[0, pl.ds(pl.multiple_of(core * 256, 256), 256), :] = product(
        attn_ref[0], grads
    ).astype(jnp.bfloat16)
    out_ref[0, pl.ds(pl.multiple_of((1 - core) * 256, 256), 256), :] = (
        product(got_ref[0, :rows], grads[rows:]) + product(got_ref[0, rows:], grads[:rows])
    ).astype(jnp.bfloat16)


def add_last_terms(spots, attn, got, grads, terms):
    _, rows, width = attn.shape
    return pl.pallas_call(
        last_terms_kernel,
        grid_spec=pltpu.PrefetchScalarGridSpec(
            num_scalar_prefetch=1,
            grid=(4,),
            in_specs=[
                pl.BlockSpec((1, rows, width), lambda i, spots: (i // 2, 0, 0)),
                pl.BlockSpec((1, rows, width), lambda i, spots: (i // 2, 0, 0)),
                pl.BlockSpec((rows, 256), lambda i, spots: (0, i % 2)),
                pl.BlockSpec(memory_space=pl.ANY),
            ],
            out_specs=pl.BlockSpec((1, 512, 256), lambda i, spots: (spots[12 + i], 0, 0)),
        ),
        out_shape=jax.ShapeDtypeStruct(terms.shape, terms.dtype),
        input_output_aliases={4: 0},
        cost_estimate=cost(2 * rows * 1024 * 512, 4 * 2**20),
        compiler_params=LIMIT,
    )(spots, attn, got, grads, terms)


def hidden_grad_kernel(table_ref, grad_ref, w0, w1, w2, w3, normed_ref, *rest):
    out_ref, gain_ref, bias_ref, total_ref = rest[-4:]
    for i in range(3):
        bias_ref[i] = jnp.sum(grad_ref[i].astype(jnp.float32), 0, keepdims=True)
    total_ref[...] = jnp.zeros(total_ref.shape, jnp.float32)

    def visit(block, low_y, ref):
        @pl.when(block < 6)
        def _():
            columns = pl.ds(pl.multiple_of(block % 2 * 256, 256), 256)
            total_ref[low_y] += lax.dot_general(
                grad_ref[block // 2, :, columns],
                ref[...],
                (((1,), (1,)), ((), ())),
                preferred_element_type=jnp.float32,
            )

    each_unit(table_ref, (w0, w1, w2, w3), visit)
    for z in range(8):
        for low_y in range(2):
            at_row = (z * 2 + low_y) * 64
            out_ref[:, at_row : at_row + 64] = total_ref[low_y, :, z * 64 : (z + 1) * 64]
    gain_ref[...] = jnp.sum(out_ref[...] * normed_ref[...], 0, keepdims=True)


def find_hidden_grad(table, grad_qkv, weights, normed, after):
    rows, width = normed.shape
    return pl.pallas_call(
        hidden_grad_kernel,
        in_specs=[SMEM] + [VMEM] * 6 + [pl.BlockSpec(memory_space=pl.ANY)] * len(after),
        out_specs=[VMEM] * 3,
        out_shape=[
            jax.ShapeDtypeStruct((rows, width), jnp.float32),
            jax.ShapeDtypeStruct((1, width), jnp.float32),
            jax.ShapeDtypeStruct((3, 1, width // 2), jnp.float32),
        ],
        scratch_shapes=[pltpu.VMEM((2, rows, width // 2), jnp.float32)],
        cost_estimate=cost(2 * rows * width * 1536, 14 * 2**20),
        compiler_params=LARGE,
    )(table, grad_qkv, *weights, normed, *after)


def per_device(inputs, grad_out, fluid, w_qkv, qkv_bias, w_proj, ln_gain):
    full, low = jnp.float32, jnp.bfloat16
    width = w_proj.shape[1]
    half = width // 2
    x, y, z, core = places()
    first = core == 0
    own_rows = w_qkv.shape[0]
    n_space = lax.axis_size("space")
    zero = jnp.uint32(0)

    def block_of(x, y):
        return jnp.where(first, x * 2 + (y >> 1), (y >> 1) * 4 + x)

    def unit_of(outer, inner):
        return (
            jnp.where(first, outer, (outer & 2) + (inner >> 1)),
            jnp.where(first, inner >> 1, inner & 1),
            jnp.where(first, inner, outer) & 1,
        )

    inner_at, outer_at = jnp.where(first, y, x), jnp.where(first, x, y)
    steps4 = jnp.arange(4, dtype=jnp.uint32)
    block, side, low_y = unit_of((outer_at - steps4[:, None]) & 3, (inner_at - steps4[None]) & 3)
    table = jnp.concatenate(
        [
            (block * 2 + side).reshape(-1),
            jnp.broadcast_to(low_y, (4, 4)).reshape(-1),
            core.reshape(1),
        ]
    ).astype(jnp.int32)
    low_y = jnp.array([i // 6 for i in range(12)] + [i // 2 for i in range(4)], jnp.uint32)
    block = jnp.array([i % 6 for i in range(12)] + [6 + i % 2 for i in range(4)], jnp.uint32)
    block, side = block >> 1, block & 1
    outer_to = jnp.where(first, block, low_y + (block & 2))
    inner_to = jnp.where(first, low_y + 2 * side, (block & 1) * 2 + side)
    spots = ((outer_to - outer_at) & 3) * 4 + ((inner_to - inner_at) & 3)
    spots = jnp.concatenate([spots, core.reshape(1)]).astype(jnp.int32)

    def back(block):
        return lax.ppermute(block, "space", [((i + 1) % n_space, i) for i in range(n_space)])

    walls_plane = jnp.pad(
        fluid[:SHIFT].transpose(1, 2, 0).astype(low), ((0, 0), (0, 0), (0, width - SHIFT))
    )
    rims = back(
        jnp.concatenate([inputs[:, :SHIFT], grad_out[:, :SHIFT], walls_plane[None, None]], 1)
    )
    qkv_parts = w_qkv.reshape(own_rows, 3, 2, half)
    mine = jnp.concatenate(
        [jnp.where(first, qkv_parts[:, i, 0], qkv_parts[:, i, 1]) for i in range(3)]
        + [jnp.where(first, w_proj[:, :half], w_proj[:, half:])],
        1,
    )
    share = lax.dynamic_slice(mine, (zero, block_of(x, y) * 256), (own_rows, 256))
    lined = trade_z(jnp.broadcast_to(share, (8, own_rows, 256)))
    quarters = jnp.stack([lined] + [crossed(lined, d, 1) for d in range(1, 4)])
    rim_x, rim_g = rims[:, :SHIFT], rims[:, SHIFT : 2 * SHIFT]
    rim_f = rims[0, 2 * SHIFT, :, :, :SHIFT].transpose(2, 0, 1).astype(fluid.dtype)
    tile_x = jnp.roll(jnp.concatenate([inputs[:, SHIFT:], rim_x], 1), (-SHIFT, -SHIFT), (2, 3))
    tile_g = jnp.roll(jnp.concatenate([grad_out[:, SHIFT:], rim_g], 1), (-SHIFT, -SHIFT), (2, 3))
    tile_f = jnp.roll(jnp.concatenate([fluid[SHIFT:], rim_f], 0), (-SHIFT, -SHIFT), (1, 2))
    extra = ((0, ROWS - TOKENS), (0, 0))
    rows_x = jnp.pad(tile_x.reshape(-1, width), extra)
    rows_g = jnp.pad(tile_g.reshape(-1, width), extra)
    both_x = jnp.concatenate([rows_x, swap(rows_x)], 0).astype(full)
    walls_row = jnp.pad(tile_f.reshape(1, -1).astype(low), ((0, 0), (0, width - TOKENS)))
    padding = jnp.zeros((ROWS - TOKENS - 1, width), low)
    got_g = swap(jnp.concatenate([tile_g.reshape(-1, width), walls_row, padding], 0))
    other_f = got_g[TOKENS, :TOKENS].astype(fluid.dtype)
    grads = jnp.concatenate([rows_g, jnp.pad(got_g[:TOKENS], extra)], 0)
    average = jnp.mean(both_x, -1, keepdims=True)
    centred = both_x - average
    variance = jnp.mean(centred * centred, -1, keepdims=True)
    inv_std = 1.0 / jnp.sqrt(variance + EPS)
    normed = centred * inv_std
    hidden = (normed * ln_gain).astype(low)
    hidden_by = hidden.reshape(2 * ROWS, 8, 2, own_rows).transpose(2, 0, 1, 3)
    hidden_by = hidden_by.reshape(2, 2 * ROWS, half)
    hidden_t = hidden_by.transpose(0, 2, 1)
    grads_own_first = jnp.where(
        first, grads, jnp.concatenate([grads[:, half:], grads[:, :half]], 1)
    )

    steps = jnp.arange(WIN, dtype=jnp.int32)
    inner = jnp.where(steps < WIN - SHIFT, 1, 2).astype(jnp.int32)
    last_pair = (x == 3) & (y >= 2)

    def masked(walls, is_last):
        along = jnp.where(is_last, inner, 0)
        labels = along[:, None, None] * 9 + inner[None, :, None] * 3 + inner[None, None, :]
        labels = jnp.pad(labels.reshape(-1), (0, ROWS - TOKENS), constant_values=-1)
        open_keys = jnp.pad(walls.reshape(-1) == 1, (0, ROWS - TOKENS))
        allowed = (labels[:, None] == labels[None, :]) & (
            open_keys[:, None] | jnp.eye(ROWS, dtype=bool)
        )
        return jnp.where(allowed, 0.0, NEG).astype(full)

    mask = jnp.stack([masked(tile_f, last_pair & ~first), masked(other_f, last_pair & first)])

    biases = qkv_bias.reshape(3, 2, half)
    biases = jnp.where(first, biases[:, 0], biases[:, 1]).reshape(6, 1, 256)
    weights = [quarters] + [crossed(quarters, d, 0) for d in range(1, 4)]
    weights[1] = follow(
        weights[1], (hidden_t, hidden_by, normed, mask, grads_own_first, biases, table, spots)
    )
    weights = [piece.reshape(4, half, 256) for piece in weights]
    kept, sent = pick(table, weights)
    got = swap(sent)
    qkv = project(table, hidden_by, weights, biases)
    dout = find_dout(grads_own_first, kept, got)
    attn, grad_qkv = attend(qkv, dout, mask)

    terms = add_last_terms(
        spots, attn, swap(attn), grads_own_first, find_terms(spots, hidden_t, grad_qkv)
    )
    pieces = terms.reshape(4, 4, 8, own_rows, 256)
    pieces = [pieces[d] for d in range(4)]
    sums = pieces[0].astype(full)
    for d in range(1, 4):
        sums = sums + crossed(pieces[d], d, 0).astype(full)
    sums = sums.astype(low)

    corners = [piece[0, 0, :16, :128] for piece in pieces[1:]]
    partial, gain_term, bias_term = find_hidden_grad(
        table, grad_qkv, weights, normed, corners
    )
    bias_term = bias_term.reshape(3, 1, half)
    nothing = jnp.zeros_like(bias_term)
    bias_term = jnp.where(
        first,
        jnp.concatenate([bias_term, nothing], 1),
        jnp.concatenate([nothing, bias_term], 1),
    )
    small = jnp.concatenate([gain_term.reshape(-1), bias_term.reshape(-1)]).reshape(16, 256)
    small = small + swap(small)

    def split(values):
        upper = lax.reduce_precision(values, 8, 7)
        return jnp.concatenate([upper.astype(low), (values - upper).astype(low)], 0)

    def joined(rows):
        return rows[-32:-16].astype(full) + rows[-16:].astype(full)

    def with_small(rows, extra_rows):
        return jnp.concatenate([rows.reshape(-1, 256), extra_rows], 0)

    extra_rows = split(small)
    total = sums[0].reshape(-1, 256).astype(full)
    for d in range(1, 4):
        arrived = crossed(with_small(sums[d], extra_rows), d, 1)
        total = total + arrived[:-32].astype(full)
        small = small + joined(arrived)
    sums = total.astype(low).reshape(8, own_rows, 256)
    repeated = jnp.broadcast_to(small.astype(low), (8, 16, 256))
    arrived = trade_z(jnp.concatenate([sums, repeated], 1))
    final = jnp.sum(arrived.astype(full), 0).astype(low)
    arrived = trade_space(jnp.broadcast_to(final, (8, own_rows + 16, 256)))
    small = jnp.sum(arrived[:4, own_rows:].astype(full), 0)
    rows = arrived[:, :own_rows]
    rows = jnp.where(
        first, rows.reshape(2, 4, own_rows, 256).swapaxes(0, 1).reshape(rows.shape), rows
    )
    others = swap(rows)
    small_got = swap(small)
    small = jnp.where(first, small, small_got).reshape(-1)
    sides = (jnp.where(first, rows, others), jnp.where(first, others, rows))
    blocks = [side[2 * i + j].astype(full) for i in range(4) for side in sides for j in range(2)]
    out_qkv = jnp.concatenate(blocks[:12], 1)
    out_proj = jnp.concatenate(blocks[12:], 1)

    grad_hidden = partial[:ROWS] + swap(partial[ROWS:])
    grad_norm = grad_hidden * ln_gain
    own_normed = normed[:ROWS]
    grad_flat = rows_g.astype(full) + inv_std[:ROWS] * (
        grad_norm
        - jnp.mean(grad_norm, -1, keepdims=True)
        - own_normed * jnp.mean(grad_norm * own_normed, -1, keepdims=True)
    )
    grad_tile = jnp.roll(
        grad_flat[:TOKENS].astype(low).reshape(tile_x.shape), (SHIFT, SHIFT), (2, 3)
    )
    returned = lax.ppermute(
        grad_tile[:, WIN - SHIFT :], "space", [(i, (i + 1) % n_space) for i in range(n_space)]
    )
    grad_input = jnp.concatenate([returned, grad_tile[:, : WIN - SHIFT]], 1)
    return (grad_input, out_qkv, out_proj, small[:width], small[width:])


def solution(mesh):
    tokens = P("batch", "space", None, None, None)
    return jax.shard_map(
        per_device,
        mesh=mesh,
        in_specs=(tokens, tokens, P("space", None, None), P("batch", None), P(), P("batch", None), P()),
        out_specs=(tokens, P("batch", None), P("batch", None), P(), P()),
        check_vma=False,
    )
```

```python
import itertools
import math

import jax
import jax.numpy as jnp
from jax import lax
from jax.experimental import pallas as pl
from jax.experimental.pallas import tpu as pltpu
from jax.sharding import PartitionSpec as P

HEADS = 16
WIN = 7
SHIFT = 3
TOKENS = WIN**3
ROWS = 352
EPS = 1e-05
NEG = -1e30
BOTH = ("space", "batch")


def flat(x, y, z, c):
    return ((y // 2 * 4 + x) * 2 + c) * 16 + z * 2 + y % 2


def places():
    s = lax.axis_index("space").astype(jnp.uint32)
    b = lax.axis_index("batch").astype(jnp.uint32)
    return (s >> 1) & 3, (s >> 3) * 2 + (b & 1), b >> 1, s & 1


def route(where):
    every = itertools.product(range(4), range(4), range(8), range(2))
    return [(flat(*at), flat(*where(*at))) for at in every]


def swap(block):
    return lax.ppermute(block, BOTH, route(lambda x, y, z, c: (x, y, z, 1 - c)))


def crossed(block, d, swapped):
    def where(x, y, z, c):
        if c == swapped:
            return ((x + d) % 4, y, z, c)
        return (x, (y + d) % 4, z, c)

    return lax.ppermute(block, BOTH, route(where))


def trade_z(blocks):
    groups = [[z * 2 + low_y for z in range(8)] for low_y in range(2)]
    return lax.all_to_all(blocks, "batch", 0, 0, tiled=True, axis_index_groups=groups)


def trade_space(blocks):
    groups = [[chip * 2 + c for chip in range(8)] for c in range(2)]
    return lax.all_to_all(blocks, "space", 0, 0, tiled=True, axis_index_groups=groups)


def attention_kernel(q_ref, k_ref, v_ref, g_ref, mask_ref, attn_ref, grad_ref):
    full = jnp.float32
    size = 64
    scale = 1.0 / math.sqrt(size)
    over_rows = (((0,), (0,)), ((), ()))
    over_columns = (((1,), (1,)), ((), ()))
    mask = mask_ref[0]
    for_queries = []
    for head in range(4):
        part = slice(head * size, (head + 1) * size)
        q, k, v, g = q_ref[:, part], k_ref[:, part], v_ref[:, part], g_ref[:, part]
        scaled = q * jnp.bfloat16(scale)
        scores = lax.dot_general(k, scaled, over_columns, preferred_element_type=full) + mask
        exponent = jnp.exp(scores - jnp.max(scores, 0, keepdims=True))
        probability = exponent * (1.0 / jnp.sum(exponent, 0, keepdims=True))
        low = probability.astype(jnp.bfloat16)
        grad = lax.dot_general(v, g, over_columns, preferred_element_type=full)
        centre = jnp.sum(probability * grad, 0, keepdims=True)
        score_low = (probability * (grad - centre)).astype(jnp.bfloat16)
        attn_t = lax.dot_general(v, low, over_rows, preferred_element_type=full)
        grad_q_t = lax.dot_general(k, score_low, over_rows, preferred_element_type=full) * scale
        for_queries.append((attn_t.astype(jnp.bfloat16), grad_q_t.astype(jnp.bfloat16)))
        grad_ref[1, :, part] = (
            jnp.dot(score_low, q, preferred_element_type=full) * scale
        ).astype(jnp.bfloat16)
        grad_ref[2, :, part] = jnp.dot(low, g, preferred_element_type=full).astype(jnp.bfloat16)
    for parity in range(2):
        attn_ref[parity] = jnp.concatenate(
            [attn for attn, _ in for_queries[parity::2]], 0
        ).T
    grad_ref[0] = jnp.concatenate([grad for _, grad in for_queries], 0).T


def attend(qkv, dout, mask):
    rows, width = dout.shape
    groups = width // 256

    def columns(offset):
        return pl.BlockSpec((ROWS, 256), lambda w, j: (w, offset + j))

    work = 2 * groups * 4
    return pl.pallas_call(
        attention_kernel,
        grid=(2, groups),
        in_specs=[
            columns(0),
            columns(groups),
            columns(2 * groups),
            columns(0),
            pl.BlockSpec((1, ROWS, ROWS), lambda w, j: (w, 0, 0)),
        ],
        out_specs=[
            pl.BlockSpec((2, ROWS, 128), lambda w, j: (0, w, j)),
            pl.BlockSpec((3, ROWS, 256), lambda w, j: (0, w, j)),
        ],
        out_shape=[
            jax.ShapeDtypeStruct((2, rows, width // 2), jnp.bfloat16),
            jax.ShapeDtypeStruct((3, rows, width), jnp.bfloat16),
        ],
        cost_estimate=pl.CostEstimate(
            flops=work * 14 * ROWS * ROWS * 64 * 4,
            bytes_accessed=8 * rows * width * 2,
            transcendentals=work * ROWS * ROWS,
        ),
        compiler_params=pltpu.CompilerParams(vmem_limit_bytes=24 * 2**20),
    )(qkv, qkv, qkv, dout, mask)


SMALL = pltpu.CompilerParams(vmem_limit_bytes=2**20)
LIMIT = pltpu.CompilerParams(vmem_limit_bytes=20 * 2**20)
LARGE = pltpu.CompilerParams(vmem_limit_bytes=30 * 2**20)


def cost(flops, bytes_accessed):
    return pl.CostEstimate(flops=flops, bytes_accessed=bytes_accessed, transcendentals=0)


def follow(array, after):
    return pl.pallas_call(
        lambda *refs: None,
        in_specs=[pl.BlockSpec(memory_space=pl.ANY)] * (1 + len(after)),
        out_specs=pl.BlockSpec(memory_space=pl.ANY),
        out_shape=jax.ShapeDtypeStruct(array.shape, array.dtype),
        input_output_aliases={0: 0},
        cost_estimate=cost(0, 0),
        compiler_params=SMALL,
    )(array, *after)


SMEM = pl.BlockSpec(memory_space=pltpu.SMEM)
VMEM = pl.BlockSpec(memory_space=pltpu.VMEM)


def norm_kernel(own_ref, got_ref, gain_ref, normed_ref, by_ref, t_ref, inv_ref):
    for i, ref in enumerate((own_ref, got_ref)):
        rows = ref[...].astype(jnp.float32)
        part = slice(i * ROWS, (i + 1) * ROWS)
        centred = rows - jnp.mean(rows, -1, keepdims=True)
        variance = jnp.mean(centred * centred, -1, keepdims=True)
        inv_std = 1.0 / jnp.sqrt(variance + EPS)
        normed = centred * inv_std
        hidden = (normed * gain_ref[...]).astype(jnp.bfloat16)
        normed_ref[part, :] = normed
        inv_ref[part, :] = inv_std
        for z in range(8):
            for low_y in range(2):
                column = (z * 2 + low_y) * 64
                by_ref[low_y, part, z * 64 : (z + 1) * 64] = hidden[:, column : column + 64]
    for low_y in range(2):
        t_ref[low_y] = by_ref[low_y].T


def normalise(own, got, gain):
    rows, width = own.shape
    return pl.pallas_call(
        norm_kernel,
        in_specs=[VMEM] * 3,
        out_specs=[VMEM] * 4,
        out_shape=[
            jax.ShapeDtypeStruct((2 * rows, width), jnp.float32),
            jax.ShapeDtypeStruct((2, 2 * rows, width // 2), jnp.bfloat16),
            jax.ShapeDtypeStruct((2, width // 2, 2 * rows), jnp.bfloat16),
            jax.ShapeDtypeStruct((2 * rows, 1), jnp.float32),
        ],
        cost_estimate=cost(0, 0),
        compiler_params=LIMIT,
    )(own, got, gain)


def collect_kernel(spots_ref, w0, w1, w2, w3, held_ref, kept_ref, sent_ref, sems):
    core = spots_ref[16]
    copies = [
        pltpu.make_async_copy(ref, held_ref.at[pl.ds(4 * d, 4)], sems.at[d])
        for d, ref in enumerate((w0, w1, w2, w3))
    ]
    for copy in copies:
        copy.start()
    for copy in copies:
        copy.wait()
    for i in range(4):
        spot = spots_ref[12 + i]
        kept_ref[i] = held_ref[spot, pl.ds(pl.multiple_of(core * 256, 256), 256), :]
        sent_ref[i] = held_ref[spot, pl.ds(pl.multiple_of((1 - core) * 256, 256), 256), :]


def collect(spots, weights):
    anywhere = pl.BlockSpec(memory_space=pl.ANY)
    return pl.pallas_call(
        collect_kernel,
        in_specs=[SMEM] + [anywhere] * 4,
        out_specs=[VMEM] * 3,
        out_shape=[jax.ShapeDtypeStruct((16, 512, 256), jnp.bfloat16)]
        + [jax.ShapeDtypeStruct((4, 256, 256), jnp.bfloat16)] * 2,
        scratch_shapes=[pltpu.SemaphoreType.DMA((4,))],
        cost_estimate=cost(0, 8 * 2**20),
        compiler_params=LIMIT,
    )(spots, *weights)


def project_kernel(spots_ref, hidden_ref, held_ref, bias_ref, out_ref):
    for block in range(6):
        total = bias_ref[block]
        for low_y in range(2):
            total = total + jnp.dot(
                hidden_ref[low_y],
                held_ref[spots_ref[low_y * 6 + block]],
                preferred_element_type=jnp.float32,
            )
        out_ref[:, block * 256 : (block + 1) * 256] = total.astype(jnp.bfloat16)


def project(spots, hidden, held, biases):
    rows = hidden.shape[1]
    return pl.pallas_call(
        project_kernel,
        in_specs=[SMEM] + [VMEM] * 3,
        out_specs=VMEM,
        out_shape=jax.ShapeDtypeStruct((rows, 1536), jnp.bfloat16),
        cost_estimate=cost(2 * rows * 1024 * 1536, 8 * 2**20),
        compiler_params=LIMIT,
    )(spots, hidden, held, biases)


def dout_kernel(grad_ref, kept_ref, got_ref, out_ref):
    for low_y in range(2):
        total = 0.0
        for i in range(4):
            ref = kept_ref if i < 2 else got_ref
            total = total + lax.dot_general(
                grad_ref[:, i * 256 : (i + 1) * 256],
                ref[low_y * 2 + i % 2],
                (((1,), (1,)), ((), ())),
                preferred_element_type=jnp.float32,
            )
        total = total.astype(jnp.bfloat16)
        for i in range(4):
            head = 2 * i + low_y
            out_ref[:, head * 64 : (head + 1) * 64] = total[:, i * 64 : (i + 1) * 64]


def find_dout(grads, kept, got):
    rows = grads.shape[0]
    return pl.pallas_call(
        dout_kernel,
        in_specs=[VMEM] * 3,
        out_specs=VMEM,
        out_shape=jax.ShapeDtypeStruct((rows, 512), jnp.bfloat16),
        cost_estimate=cost(2 * rows * 1024 * 512, 4 * 2**20),
        compiler_params=LIMIT,
    )(grads, kept, got)


def terms_kernel(spots_ref, left_ref, right_ref, out_ref):
    for low_y in range(2):
        left = left_ref[low_y]
        for block in range(6):
            right = right_ref[block // 2, :, block % 2 * 256 : (block % 2 + 1) * 256]
            out_ref[spots_ref[low_y * 6 + block]] = jnp.dot(
                left, right, preferred_element_type=jnp.float32
            ).astype(jnp.bfloat16)


def find_terms(spots, hidden_t, grad_qkv):
    _, half, rows = hidden_t.shape
    return pl.pallas_call(
        terms_kernel,
        in_specs=[SMEM] + [VMEM] * 2,
        out_specs=VMEM,
        out_shape=jax.ShapeDtypeStruct((16, half, 256), jnp.bfloat16),
        cost_estimate=cost(2 * rows * half * 3072, 8 * 2**20),
        compiler_params=LIMIT,
    )(spots, hidden_t, grad_qkv)


def last_terms_kernel(spots_ref, attn_ref, got_ref, grads_ref, terms_ref, out_ref):
    core = spots_ref[16]
    rows = grads_ref.shape[0] // 2
    grads = grads_ref[...]

    def product(left, right):
        return lax.dot_general(
            left, right, (((0,), (0,)), ((), ())), preferred_element_type=jnp.float32
        )

    out_ref[0, pl.ds(pl.multiple_of(core * 256, 256), 256), :] = product(
        attn_ref[0], grads
    ).astype(jnp.bfloat16)
    out_ref[0, pl.ds(pl.multiple_of((1 - core) * 256, 256), 256), :] = (
        product(got_ref[0, :rows], grads[rows:]) + product(got_ref[0, rows:], grads[:rows])
    ).astype(jnp.bfloat16)


def add_last_terms(spots, attn, got, grads, terms):
    _, rows, width = attn.shape
    return pl.pallas_call(
        last_terms_kernel,
        grid_spec=pltpu.PrefetchScalarGridSpec(
            num_scalar_prefetch=1,
            grid=(4,),
            in_specs=[
                pl.BlockSpec((1, rows, width), lambda i, spots: (i // 2, 0, 0)),
                pl.BlockSpec((1, rows, width), lambda i, spots: (i // 2, 0, 0)),
                pl.BlockSpec((rows, 256), lambda i, spots: (0, i % 2)),
                pl.BlockSpec(memory_space=pl.ANY),
            ],
            out_specs=pl.BlockSpec((1, 512, 256), lambda i, spots: (spots[12 + i], 0, 0)),
        ),
        out_shape=jax.ShapeDtypeStruct(terms.shape, terms.dtype),
        input_output_aliases={4: 0},
        cost_estimate=cost(2 * rows * 1024 * 512, 4 * 2**20),
        compiler_params=LIMIT,
    )(spots, attn, got, grads, terms)


def hidden_grad_kernel(spots_ref, grad_ref, held_ref, normed_ref, *rest):
    out_ref, gain_ref, bias_ref = rest[-3:]
    for i in range(3):
        bias_ref[i] = jnp.sum(grad_ref[i].astype(jnp.float32), 0, keepdims=True)
    for low_y in range(2):
        total = 0.0
        for block in range(6):
            total = total + lax.dot_general(
                grad_ref[block // 2, :, block % 2 * 256 : (block % 2 + 1) * 256],
                held_ref[spots_ref[low_y * 6 + block]],
                (((1,), (1,)), ((), ())),
                preferred_element_type=jnp.float32,
            )
        for z in range(8):
            column = (z * 2 + low_y) * 64
            out_ref[:, column : column + 64] = total[:, z * 64 : (z + 1) * 64]
    gain_ref[...] = jnp.sum(out_ref[...] * normed_ref[...], 0, keepdims=True)


def find_hidden_grad(spots, grad_qkv, held, normed, after):
    rows, width = normed.shape
    return pl.pallas_call(
        hidden_grad_kernel,
        in_specs=[SMEM] + [VMEM] * 3 + [pl.BlockSpec(memory_space=pl.ANY)] * len(after),
        out_specs=[VMEM] * 3,
        out_shape=[
            jax.ShapeDtypeStruct((rows, width), jnp.float32),
            jax.ShapeDtypeStruct((1, width), jnp.float32),
            jax.ShapeDtypeStruct((3, 1, width // 2), jnp.float32),
        ],
        cost_estimate=cost(2 * rows * width * 1536, 14 * 2**20),
        compiler_params=LARGE,
    )(spots, grad_qkv, held, normed, *after)


def per_device(inputs, grad_out, fluid, w_qkv, qkv_bias, w_proj, ln_gain):
    full, low = jnp.float32, jnp.bfloat16
    width = w_proj.shape[1]
    half = width // 2
    x, y, z, core = places()
    first = core == 0
    own_rows = w_qkv.shape[0]
    n_space = lax.axis_size("space")
    zero = jnp.uint32(0)

    def block_of(x, y):
        return jnp.where(first, x * 2 + (y >> 1), (y >> 1) * 4 + x)

    inner_at, outer_at = jnp.where(first, y, x), jnp.where(first, x, y)
    low_y = jnp.array([i // 6 for i in range(12)] + [i // 2 for i in range(4)], jnp.uint32)
    block = jnp.array([i % 6 for i in range(12)] + [6 + i % 2 for i in range(4)], jnp.uint32)
    block, side = block >> 1, block & 1
    outer_to = jnp.where(first, block, low_y + (block & 2))
    inner_to = jnp.where(first, low_y + 2 * side, (block & 1) * 2 + side)
    spots = ((outer_to - outer_at) & 3) * 4 + ((inner_to - inner_at) & 3)
    spots = jnp.concatenate([spots, core.reshape(1)]).astype(jnp.int32)
    table = ((outer_at - outer_to) & 3) * 4 + ((inner_at - inner_to) & 3)
    table = jnp.concatenate([table, core.reshape(1)]).astype(jnp.int32)

    def back(block):
        return lax.ppermute(block, "space", [((i + 1) % n_space, i) for i in range(n_space)])

    walls_plane = jnp.pad(
        fluid[:SHIFT].transpose(1, 2, 0).astype(low), ((0, 0), (0, 0), (0, width - SHIFT))
    )
    rims = back(
        jnp.concatenate([inputs[:, :SHIFT], grad_out[:, :SHIFT], walls_plane[None, None]], 1)
    )
    qkv_parts = w_qkv.reshape(own_rows, 3, 2, half)
    mine = jnp.concatenate(
        [jnp.where(first, qkv_parts[:, i, 0], qkv_parts[:, i, 1]) for i in range(3)]
        + [jnp.where(first, w_proj[:, :half], w_proj[:, half:])],
        1,
    )
    share = lax.dynamic_slice(mine, (zero, block_of(x, y) * 256), (own_rows, 256))
    lined = trade_z(jnp.broadcast_to(share, (8, own_rows, 256)))
    quarters = jnp.stack([lined] + [crossed(lined, d, 1) for d in range(1, 4)])
    rim_x, rim_g = rims[:, :SHIFT], rims[:, SHIFT : 2 * SHIFT]
    rim_f = rims[0, 2 * SHIFT, :, :, :SHIFT].transpose(2, 0, 1).astype(fluid.dtype)
    tile_x = jnp.roll(jnp.concatenate([inputs[:, SHIFT:], rim_x], 1), (-SHIFT, -SHIFT), (2, 3))
    tile_g = jnp.roll(jnp.concatenate([grad_out[:, SHIFT:], rim_g], 1), (-SHIFT, -SHIFT), (2, 3))
    tile_f = jnp.roll(jnp.concatenate([fluid[SHIFT:], rim_f], 0), (-SHIFT, -SHIFT), (1, 2))
    extra = ((0, ROWS - TOKENS), (0, 0))
    rows_x = jnp.pad(tile_x.reshape(-1, width), extra)
    rows_g = jnp.pad(tile_g.reshape(-1, width), extra)
    normed, hidden_by, hidden_t, inv_std = normalise(
        rows_x, swap(rows_x), ln_gain.reshape(1, width)
    )
    walls_row = jnp.pad(tile_f.reshape(1, -1).astype(low), ((0, 0), (0, width - TOKENS)))
    padding = jnp.zeros((ROWS - TOKENS - 1, width), low)
    got_g = swap(jnp.concatenate([tile_g.reshape(-1, width), walls_row, padding], 0))
    other_f = got_g[TOKENS, :TOKENS].astype(fluid.dtype)
    grads = jnp.concatenate([rows_g, jnp.pad(got_g[:TOKENS], extra)], 0)
    grads_own_first = jnp.where(
        first, grads, jnp.concatenate([grads[:, half:], grads[:, :half]], 1)
    )

    steps = jnp.arange(WIN, dtype=jnp.int32)
    inner = jnp.where(steps < WIN - SHIFT, 1, 2).astype(jnp.int32)
    last_pair = (x == 3) & (y >= 2)

    def masked(walls, is_last):
        along = jnp.where(is_last, inner, 0)
        labels = along[:, None, None] * 9 + inner[None, :, None] * 3 + inner[None, None, :]
        labels = jnp.pad(labels.reshape(-1), (0, ROWS - TOKENS), constant_values=-1)
        open_keys = jnp.pad(walls.reshape(-1) == 1, (0, ROWS - TOKENS))
        allowed = (labels[:, None] == labels[None, :]) & (
            open_keys[:, None] | jnp.eye(ROWS, dtype=bool)
        )
        return jnp.where(allowed, 0.0, NEG).astype(full)

    mask = jnp.stack([masked(tile_f, last_pair & ~first), masked(other_f, last_pair & first)])

    biases = qkv_bias.reshape(3, 2, half)
    biases = jnp.where(first, biases[:, 0], biases[:, 1]).reshape(6, 1, 256)
    weights = [quarters] + [crossed(quarters, d, 0) for d in range(1, 4)]
    weights[1] = follow(
        weights[1], (hidden_t, hidden_by, normed, mask, grads_own_first, biases, table, spots)
    )
    weights = [piece.reshape(4, half, 256) for piece in weights]
    held, kept, sent = collect(table, weights)
    got = swap(sent)
    qkv = project(table, hidden_by, held, biases)
    dout = find_dout(grads_own_first, kept, got)
    attn, grad_qkv = attend(qkv, dout, mask)

    terms = add_last_terms(
        spots, attn, swap(attn), grads_own_first, find_terms(spots, hidden_t, grad_qkv)
    )
    pieces = terms.reshape(4, 4, 8, own_rows, 256)
    pieces = [pieces[d] for d in range(4)]
    sums = pieces[0].astype(full)
    for d in range(1, 4):
        sums = sums + crossed(pieces[d], d, 0).astype(full)
    sums = sums.astype(low)

    corners = [piece[0, 0, :16, :128] for piece in pieces[1:]]
    partial, gain_term, bias_term = find_hidden_grad(
        table, grad_qkv, held, normed, corners
    )
    bias_term = bias_term.reshape(3, 1, half)
    nothing = jnp.zeros_like(bias_term)
    bias_term = jnp.where(
        first,
        jnp.concatenate([bias_term, nothing], 1),
        jnp.concatenate([nothing, bias_term], 1),
    )
    small = jnp.concatenate([gain_term.reshape(-1), bias_term.reshape(-1)]).reshape(16, 256)
    small = small + swap(small)

    def split(values):
        upper = lax.reduce_precision(values, 8, 7)
        return jnp.concatenate([upper.astype(low), (values - upper).astype(low)], 0)

    def joined(rows):
        return rows[-32:-16].astype(full) + rows[-16:].astype(full)

    def with_small(rows, extra_rows):
        return jnp.concatenate([rows.reshape(-1, 256), extra_rows], 0)

    extra_rows = split(small)
    total = sums[0].reshape(-1, 256).astype(full)
    for d in range(1, 4):
        arrived = crossed(with_small(sums[d], extra_rows), d, 1)
        total = total + arrived[:-32].astype(full)
        small = small + joined(arrived)
    sums = total.astype(low).reshape(8, own_rows, 256)
    repeated = jnp.broadcast_to(small.astype(low), (8, 16, 256))
    arrived = trade_z(jnp.concatenate([sums, repeated], 1))
    final = jnp.sum(arrived.astype(full), 0).astype(low)
    arrived = trade_space(jnp.broadcast_to(final, (8, own_rows + 16, 256)))
    small = jnp.sum(arrived[:4, own_rows:].astype(full), 0)
    rows = arrived[:, :own_rows]
    rows = jnp.where(
        first, rows.reshape(2, 4, own_rows, 256).swapaxes(0, 1).reshape(rows.shape), rows
    )
    others = swap(rows)
    small_got = swap(small)
    small = jnp.where(first, small, small_got).reshape(-1)
    sides = (jnp.where(first, rows, others), jnp.where(first, others, rows))
    blocks = [side[2 * i + j].astype(full) for i in range(4) for side in sides for j in range(2)]
    out_qkv = jnp.concatenate(blocks[:12], 1)
    out_proj = jnp.concatenate(blocks[12:], 1)

    grad_hidden = partial[:ROWS] + swap(partial[ROWS:])
    grad_norm = grad_hidden * ln_gain
    own_normed = normed[:ROWS]
    grad_flat = rows_g.astype(full) + inv_std[:ROWS] * (
        grad_norm
        - jnp.mean(grad_norm, -1, keepdims=True)
        - own_normed * jnp.mean(grad_norm * own_normed, -1, keepdims=True)
    )
    grad_tile = jnp.roll(
        grad_flat[:TOKENS].astype(low).reshape(tile_x.shape), (SHIFT, SHIFT), (2, 3)
    )
    returned = lax.ppermute(
        grad_tile[:, WIN - SHIFT :], "space", [(i, (i + 1) % n_space) for i in range(n_space)]
    )
    grad_input = jnp.concatenate([returned, grad_tile[:, : WIN - SHIFT]], 1)
    return (grad_input, out_qkv, out_proj, small[:width], small[width:])


def solution(mesh):
    tokens = P("batch", "space", None, None, None)
    return jax.shard_map(
        per_device,
        mesh=mesh,
        in_specs=(tokens, tokens, P("space", None, None), P("batch", None), P(), P("batch", None), P()),
        out_specs=(tokens, P("batch", None), P("batch", None), P(), P()),
        check_vma=False,
    )
```

```python
import itertools
import math

import jax
import jax.numpy as jnp
from jax import lax
from jax.experimental import pallas as pl
from jax.experimental.pallas import tpu as pltpu
from jax.sharding import PartitionSpec as P

HEADS = 16
WIN = 7
SHIFT = 3
TOKENS = WIN**3
ROWS = 352
EPS = 1e-05
NEG = -1e30
BOTH = ("space", "batch")


def flat(x, y, z, c):
    return ((y // 2 * 4 + x) * 2 + c) * 16 + z * 2 + y % 2


def places():
    s = lax.axis_index("space").astype(jnp.uint32)
    b = lax.axis_index("batch").astype(jnp.uint32)
    return (s >> 1) & 3, (s >> 3) * 2 + (b & 1), b >> 1, s & 1


def route(where):
    every = itertools.product(range(4), range(4), range(8), range(2))
    return [(flat(*at), flat(*where(*at))) for at in every]


def swap(block):
    return lax.ppermute(block, BOTH, route(lambda x, y, z, c: (x, y, z, 1 - c)))


def crossed(block, d, swapped):
    def where(x, y, z, c):
        if c == swapped:
            return ((x + d) % 4, y, z, c)
        return (x, (y + d) % 4, z, c)

    return lax.ppermute(block, BOTH, route(where))


def trade_z(blocks):
    groups = [[z * 2 + low_y for z in range(8)] for low_y in range(2)]
    return lax.all_to_all(blocks, "batch", 0, 0, tiled=True, axis_index_groups=groups)


def trade_space(blocks):
    groups = [[chip * 2 + c for chip in range(8)] for c in range(2)]
    return lax.all_to_all(blocks, "space", 0, 0, tiled=True, axis_index_groups=groups)


def attention_kernel(q_ref, k_ref, v_ref, g_ref, mask_ref, attn_ref, grad_ref):
    full = jnp.float32
    size = 64
    scale = 1.0 / math.sqrt(size)
    over_rows = (((0,), (0,)), ((), ()))
    over_columns = (((1,), (1,)), ((), ()))
    mask = mask_ref[0]
    for_queries = []
    for head in range(8):
        part = slice(head * size, (head + 1) * size)
        q, k, v, g = q_ref[:, part], k_ref[:, part], v_ref[:, part], g_ref[:, part]
        scaled = q * jnp.bfloat16(scale)
        scores = lax.dot_general(k, scaled, over_columns, preferred_element_type=full) + mask
        exponent = jnp.exp(scores - jnp.max(scores, 0, keepdims=True))
        probability = exponent * (1.0 / jnp.sum(exponent, 0, keepdims=True))
        low = probability.astype(jnp.bfloat16)
        grad = lax.dot_general(v, g, over_columns, preferred_element_type=full)
        centre = jnp.sum(probability * grad, 0, keepdims=True)
        score_low = (probability * (grad - centre)).astype(jnp.bfloat16)
        attn_t = lax.dot_general(v, low, over_rows, preferred_element_type=full)
        grad_q_t = lax.dot_general(k, score_low, over_rows, preferred_element_type=full) * scale
        for_queries.append((attn_t.astype(jnp.bfloat16), grad_q_t.astype(jnp.bfloat16)))
        grad_ref[1, :, part] = (
            jnp.dot(score_low, q, preferred_element_type=full) * scale
        ).astype(jnp.bfloat16)
        grad_ref[2, :, part] = jnp.dot(low, g, preferred_element_type=full).astype(jnp.bfloat16)
    for parity in range(2):
        attn_ref[parity] = jnp.concatenate(
            [attn for attn, _ in for_queries[parity::2]], 0
        ).T
    grad_ref[0] = jnp.concatenate([grad for _, grad in for_queries], 0).T


def attend(qkv, dout, mask):
    rows, width = dout.shape
    groups = width // 512

    def columns(offset):
        return pl.BlockSpec((ROWS, 512), lambda w, j: (w, offset + j))

    work = 2 * groups * 8
    return pl.pallas_call(
        attention_kernel,
        grid=(2, groups),
        in_specs=[
            columns(0),
            columns(groups),
            columns(2 * groups),
            columns(0),
            pl.BlockSpec((1, ROWS, ROWS), lambda w, j: (w, 0, 0)),
        ],
        out_specs=[
            pl.BlockSpec((2, ROWS, 256), lambda w, j: (0, w, j)),
            pl.BlockSpec((3, ROWS, 512), lambda w, j: (0, w, j)),
        ],
        out_shape=[
            jax.ShapeDtypeStruct((2, rows, width // 2), jnp.bfloat16),
            jax.ShapeDtypeStruct((3, rows, width), jnp.bfloat16),
        ],
        cost_estimate=pl.CostEstimate(
            flops=work * 14 * ROWS * ROWS * 64 * 4,
            bytes_accessed=8 * rows * width * 2,
            transcendentals=work * ROWS * ROWS,
        ),
        compiler_params=pltpu.CompilerParams(vmem_limit_bytes=24 * 2**20),
    )(qkv, qkv, qkv, dout, mask)


SMALL = pltpu.CompilerParams(vmem_limit_bytes=2**20)
LIMIT = pltpu.CompilerParams(vmem_limit_bytes=20 * 2**20)
LARGE = pltpu.CompilerParams(vmem_limit_bytes=30 * 2**20)


def cost(flops, bytes_accessed):
    return pl.CostEstimate(flops=flops, bytes_accessed=bytes_accessed, transcendentals=0)


def follow(array, after):
    return pl.pallas_call(
        lambda *refs: None,
        in_specs=[pl.BlockSpec(memory_space=pl.ANY)] * (1 + len(after)),
        out_specs=pl.BlockSpec(memory_space=pl.ANY),
        out_shape=jax.ShapeDtypeStruct(array.shape, array.dtype),
        input_output_aliases={0: 0},
        cost_estimate=cost(0, 0),
        compiler_params=SMALL,
    )(array, *after)


SMEM = pl.BlockSpec(memory_space=pltpu.SMEM)
VMEM = pl.BlockSpec(memory_space=pltpu.VMEM)


def assemble_kernel(x_ref, g_ref, rim_ref, walls_ref, rows_x_ref, rows_g_ref, sent_ref, held_ref):
    for which, (ref, out_ref) in enumerate(((x_ref, rows_x_ref), (g_ref, rows_g_ref))):
        for i in range(WIN):
            for j in range(WIN):
                across = (j + SHIFT) % WIN
                if i + SHIFT < WIN:
                    line = ref[0, i + SHIFT, across]
                else:
                    line = rim_ref[0, which * SHIFT + i + SHIFT - WIN, across]
                line = line.astype(jnp.float32)
                row = (i * WIN + j) * WIN
                held_ref[row : row + WIN - SHIFT] = line[SHIFT:]
                held_ref[row + WIN - SHIFT : row + WIN] = line[:SHIFT]
        held_ref[TOKENS:] = jnp.zeros((ROWS - TOKENS, held_ref.shape[1]), jnp.float32)
        out_ref[...] = held_ref[...].astype(jnp.bfloat16)
    held_ref[TOKENS : TOKENS + 1] = walls_ref[...].astype(jnp.float32)
    sent_ref[...] = held_ref[...].astype(jnp.bfloat16)


def assemble(inputs, grad_out, rims, walls_row):
    width = inputs.shape[-1]
    return pl.pallas_call(
        assemble_kernel,
        in_specs=[VMEM] * 4,
        out_specs=[VMEM] * 3,
        out_shape=[jax.ShapeDtypeStruct((ROWS, width), jnp.bfloat16)] * 3,
        scratch_shapes=[pltpu.VMEM((ROWS, width), jnp.float32)],
        cost_estimate=cost(0, 0),
        compiler_params=LIMIT,
    )(inputs, grad_out, rims, walls_row)


def norm_kernel(own_ref, got_ref, gain_ref, normed_ref, by_ref, t_ref, inv_ref):
    for i, ref in enumerate((own_ref, got_ref)):
        rows = ref[...].astype(jnp.float32)
        part = slice(i * ROWS, (i + 1) * ROWS)
        centred = rows - jnp.mean(rows, -1, keepdims=True)
        variance = jnp.mean(centred * centred, -1, keepdims=True)
        inv_std = 1.0 / jnp.sqrt(variance + EPS)
        normed = centred * inv_std
        hidden = (normed * gain_ref[...]).astype(jnp.bfloat16)
        normed_ref[part, :] = normed
        inv_ref[part, :] = inv_std
        for z in range(8):
            for low_y in range(2):
                column = (z * 2 + low_y) * 64
                by_ref[low_y, part, z * 64 : (z + 1) * 64] = hidden[:, column : column + 64]
    for low_y in range(2):
        t_ref[low_y] = by_ref[low_y].T


def normalise(own, got, gain):
    rows, width = own.shape
    return pl.pallas_call(
        norm_kernel,
        in_specs=[VMEM] * 3,
        out_specs=[VMEM] * 4,
        out_shape=[
            jax.ShapeDtypeStruct((2 * rows, width), jnp.float32),
            jax.ShapeDtypeStruct((2, 2 * rows, width // 2), jnp.bfloat16),
            jax.ShapeDtypeStruct((2, width // 2, 2 * rows), jnp.bfloat16),
            jax.ShapeDtypeStruct((2 * rows, 1), jnp.float32),
        ],
        cost_estimate=cost(0, 0),
        compiler_params=LIMIT,
    )(own, got, gain)


def collect_kernel(spots_ref, w0, w1, w2, w3, held_ref, kept_ref, sent_ref, sems):
    core = spots_ref[16]
    copies = [
        pltpu.make_async_copy(ref, held_ref.at[pl.ds(4 * d, 4)], sems.at[d])
        for d, ref in enumerate((w0, w1, w2, w3))
    ]
    for copy in copies:
        copy.start()
    for copy in copies:
        copy.wait()
    for i in range(4):
        spot = spots_ref[12 + i]
        kept_ref[i] = held_ref[spot, pl.ds(pl.multiple_of(core * 256, 256), 256), :]
        sent_ref[i] = held_ref[spot, pl.ds(pl.multiple_of((1 - core) * 256, 256), 256), :]


def collect(spots, weights):
    anywhere = pl.BlockSpec(memory_space=pl.ANY)
    return pl.pallas_call(
        collect_kernel,
        in_specs=[SMEM] + [anywhere] * 4,
        out_specs=[VMEM] * 3,
        out_shape=[jax.ShapeDtypeStruct((16, 512, 256), jnp.bfloat16)]
        + [jax.ShapeDtypeStruct((4, 256, 256), jnp.bfloat16)] * 2,
        scratch_shapes=[pltpu.SemaphoreType.DMA((4,))],
        cost_estimate=cost(0, 8 * 2**20),
        compiler_params=LIMIT,
    )(spots, *weights)


def project_kernel(spots_ref, hidden_ref, held_ref, bias_ref, out_ref):
    for block in range(6):
        total = bias_ref[block]
        for low_y in range(2):
            total = total + jnp.dot(
                hidden_ref[low_y],
                held_ref[spots_ref[low_y * 6 + block]],
                preferred_element_type=jnp.float32,
            )
        out_ref[:, block * 256 : (block + 1) * 256] = total.astype(jnp.bfloat16)


def project(spots, hidden, held, biases):
    rows = hidden.shape[1]
    return pl.pallas_call(
        project_kernel,
        in_specs=[SMEM] + [VMEM] * 3,
        out_specs=VMEM,
        out_shape=jax.ShapeDtypeStruct((rows, 1536), jnp.bfloat16),
        cost_estimate=cost(2 * rows * 1024 * 1536, 8 * 2**20),
        compiler_params=LIMIT,
    )(spots, hidden, held, biases)


def dout_kernel(grad_ref, kept_ref, got_ref, out_ref):
    for low_y in range(2):
        total = 0.0
        for i in range(4):
            ref = kept_ref if i < 2 else got_ref
            total = total + lax.dot_general(
                grad_ref[:, i * 256 : (i + 1) * 256],
                ref[low_y * 2 + i % 2],
                (((1,), (1,)), ((), ())),
                preferred_element_type=jnp.float32,
            )
        total = total.astype(jnp.bfloat16)
        for i in range(4):
            head = 2 * i + low_y
            out_ref[:, head * 64 : (head + 1) * 64] = total[:, i * 64 : (i + 1) * 64]


def find_dout(grads, kept, got):
    rows = grads.shape[0]
    return pl.pallas_call(
        dout_kernel,
        in_specs=[VMEM] * 3,
        out_specs=VMEM,
        out_shape=jax.ShapeDtypeStruct((rows, 512), jnp.bfloat16),
        cost_estimate=cost(2 * rows * 1024 * 512, 4 * 2**20),
        compiler_params=LIMIT,
    )(grads, kept, got)


def terms_kernel(spots_ref, left_ref, right_ref, out_ref):
    for low_y in range(2):
        left = left_ref[low_y]
        for block in range(6):
            right = right_ref[block // 2, :, block % 2 * 256 : (block % 2 + 1) * 256]
            out_ref[spots_ref[low_y * 6 + block]] = jnp.dot(
                left, right, preferred_element_type=jnp.float32
            ).astype(jnp.bfloat16)


def find_terms(spots, hidden_t, grad_qkv):
    _, half, rows = hidden_t.shape
    return pl.pallas_call(
        terms_kernel,
        in_specs=[SMEM] + [VMEM] * 2,
        out_specs=VMEM,
        out_shape=jax.ShapeDtypeStruct((16, half, 256), jnp.bfloat16),
        cost_estimate=cost(2 * rows * half * 3072, 8 * 2**20),
        compiler_params=LIMIT,
    )(spots, hidden_t, grad_qkv)


def last_terms_kernel(spots_ref, attn_ref, got_ref, grads_ref, terms_ref, out_ref):
    core = spots_ref[16]
    rows = grads_ref.shape[0] // 2
    grads = grads_ref[...]

    def product(left, right):
        return lax.dot_general(
            left, right, (((0,), (0,)), ((), ())), preferred_element_type=jnp.float32
        )

    out_ref[0, pl.ds(pl.multiple_of(core * 256, 256), 256), :] = product(
        attn_ref[0], grads
    ).astype(jnp.bfloat16)
    out_ref[0, pl.ds(pl.multiple_of((1 - core) * 256, 256), 256), :] = (
        product(got_ref[0, :rows], grads[rows:]) + product(got_ref[0, rows:], grads[:rows])
    ).astype(jnp.bfloat16)


def add_last_terms(spots, attn, got, grads, terms):
    _, rows, width = attn.shape
    return pl.pallas_call(
        last_terms_kernel,
        grid_spec=pltpu.PrefetchScalarGridSpec(
            num_scalar_prefetch=1,
            grid=(4,),
            in_specs=[
                pl.BlockSpec((1, rows, width), lambda i, spots: (i // 2, 0, 0)),
                pl.BlockSpec((1, rows, width), lambda i, spots: (i // 2, 0, 0)),
                pl.BlockSpec((rows, 256), lambda i, spots: (0, i % 2)),
                pl.BlockSpec(memory_space=pl.ANY),
            ],
            out_specs=pl.BlockSpec((1, 512, 256), lambda i, spots: (spots[12 + i], 0, 0)),
        ),
        out_shape=jax.ShapeDtypeStruct(terms.shape, terms.dtype),
        input_output_aliases={4: 0},
        cost_estimate=cost(2 * rows * 1024 * 512, 4 * 2**20),
        compiler_params=LIMIT,
    )(spots, attn, got, grads, terms)


def hidden_grad_kernel(spots_ref, grad_ref, held_ref, normed_ref, *rest):
    out_ref, gain_ref, bias_ref = rest[-3:]
    for i in range(3):
        bias_ref[i] = jnp.sum(grad_ref[i].astype(jnp.float32), 0, keepdims=True)
    for low_y in range(2):
        total = 0.0
        for block in range(6):
            total = total + lax.dot_general(
                grad_ref[block // 2, :, block % 2 * 256 : (block % 2 + 1) * 256],
                held_ref[spots_ref[low_y * 6 + block]],
                (((1,), (1,)), ((), ())),
                preferred_element_type=jnp.float32,
            )
        for z in range(8):
            column = (z * 2 + low_y) * 64
            out_ref[:, column : column + 64] = total[:, z * 64 : (z + 1) * 64]
    gain_ref[...] = jnp.sum(out_ref[...] * normed_ref[...], 0, keepdims=True)


def find_hidden_grad(spots, grad_qkv, held, normed, after):
    rows, width = normed.shape
    return pl.pallas_call(
        hidden_grad_kernel,
        in_specs=[SMEM] + [VMEM] * 3 + [pl.BlockSpec(memory_space=pl.ANY)] * len(after),
        out_specs=[VMEM] * 3,
        out_shape=[
            jax.ShapeDtypeStruct((rows, width), jnp.float32),
            jax.ShapeDtypeStruct((1, width), jnp.float32),
            jax.ShapeDtypeStruct((3, 1, width // 2), jnp.float32),
        ],
        cost_estimate=cost(2 * rows * width * 1536, 14 * 2**20),
        compiler_params=LARGE,
    )(spots, grad_qkv, held, normed, *after)


def per_device(inputs, grad_out, fluid, w_qkv, qkv_bias, w_proj, ln_gain):
    full, low = jnp.float32, jnp.bfloat16
    width = w_proj.shape[1]
    half = width // 2
    x, y, z, core = places()
    first = core == 0
    own_rows = w_qkv.shape[0]
    n_space = lax.axis_size("space")
    zero = jnp.uint32(0)

    def block_of(x, y):
        return jnp.where(first, x * 2 + (y >> 1), (y >> 1) * 4 + x)

    inner_at, outer_at = jnp.where(first, y, x), jnp.where(first, x, y)
    low_y = jnp.array([i // 6 for i in range(12)] + [i // 2 for i in range(4)], jnp.uint32)
    block = jnp.array([i % 6 for i in range(12)] + [6 + i % 2 for i in range(4)], jnp.uint32)
    block, side = block >> 1, block & 1
    outer_to = jnp.where(first, block, low_y + (block & 2))
    inner_to = jnp.where(first, low_y + 2 * side, (block & 1) * 2 + side)
    spots = ((outer_to - outer_at) & 3) * 4 + ((inner_to - inner_at) & 3)
    spots = jnp.concatenate([spots, core.reshape(1)]).astype(jnp.int32)
    table = ((outer_at - outer_to) & 3) * 4 + ((inner_at - inner_to) & 3)
    table = jnp.concatenate([table, core.reshape(1)]).astype(jnp.int32)

    def back(block):
        return lax.ppermute(block, "space", [((i + 1) % n_space, i) for i in range(n_space)])

    walls_plane = jnp.pad(
        fluid[:SHIFT].transpose(1, 2, 0).astype(low), ((0, 0), (0, 0), (0, width - SHIFT))
    )
    rims = back(
        jnp.concatenate([inputs[:, :SHIFT], grad_out[:, :SHIFT], walls_plane[None, None]], 1)
    )
    qkv_parts = w_qkv.reshape(own_rows, 3, 2, half)
    mine = jnp.concatenate(
        [jnp.where(first, qkv_parts[:, i, 0], qkv_parts[:, i, 1]) for i in range(3)]
        + [jnp.where(first, w_proj[:, :half], w_proj[:, half:])],
        1,
    )
    share = lax.dynamic_slice(mine, (zero, block_of(x, y) * 256), (own_rows, 256))
    lined = trade_z(jnp.broadcast_to(share, (8, own_rows, 256)))
    quarters = jnp.stack([lined] + [crossed(lined, d, 1) for d in range(1, 4)])
    rims = follow(rims, (quarters[:, 0, :16, :128],))
    rim_f = rims[0, 2 * SHIFT, :, :, :SHIFT].transpose(2, 0, 1).astype(fluid.dtype)
    tile_f = jnp.roll(jnp.concatenate([fluid[SHIFT:], rim_f], 0), (-SHIFT, -SHIFT), (1, 2))
    walls_row = jnp.pad(tile_f.reshape(1, -1).astype(low), ((0, 0), (0, width - TOKENS)))
    rows_x, rows_g, sent_g = assemble(inputs, grad_out, rims, walls_row)
    normed, hidden_by, hidden_t, inv_std = normalise(
        rows_x, swap(rows_x), ln_gain.reshape(1, width)
    )
    got_g = swap(sent_g)
    other_f = got_g[TOKENS, :TOKENS].astype(fluid.dtype)
    extra = ((0, ROWS - TOKENS), (0, 0))
    grads = jnp.concatenate([rows_g, jnp.pad(got_g[:TOKENS], extra)], 0)
    grads_own_first = jnp.where(
        first, grads, jnp.concatenate([grads[:, half:], grads[:, :half]], 1)
    )

    steps = jnp.arange(WIN, dtype=jnp.int32)
    inner = jnp.where(steps < WIN - SHIFT, 1, 2).astype(jnp.int32)
    last_pair = (x == 3) & (y >= 2)

    def masked(walls, is_last):
        along = jnp.where(is_last, inner, 0)
        labels = along[:, None, None] * 9 + inner[None, :, None] * 3 + inner[None, None, :]
        labels = jnp.pad(labels.reshape(-1), (0, ROWS - TOKENS), constant_values=-1)
        open_keys = jnp.pad(walls.reshape(-1) == 1, (0, ROWS - TOKENS))
        allowed = (labels[:, None] == labels[None, :]) & (
            open_keys[:, None] | jnp.eye(ROWS, dtype=bool)
        )
        return jnp.where(allowed, 0.0, NEG).astype(full)

    mask = jnp.stack([masked(tile_f, last_pair & ~first), masked(other_f, last_pair & first)])

    biases = qkv_bias.reshape(3, 2, half)
    biases = jnp.where(first, biases[:, 0], biases[:, 1]).reshape(6, 1, 256)
    weights = [quarters] + [crossed(quarters, d, 0) for d in range(1, 4)]
    weights[1] = follow(
        weights[1], (hidden_t, hidden_by, normed, mask, grads_own_first, biases, table, spots)
    )
    weights = [piece.reshape(4, half, 256) for piece in weights]
    held, kept, sent = collect(table, weights)
    got = swap(sent)
    qkv = project(table, hidden_by, held, biases)
    dout = find_dout(grads_own_first, kept, got)
    attn, grad_qkv = attend(qkv, dout, mask)

    terms = add_last_terms(
        spots, attn, swap(attn), grads_own_first, find_terms(spots, hidden_t, grad_qkv)
    )
    pieces = terms.reshape(4, 4, 8, own_rows, 256)
    pieces = [pieces[d] for d in range(4)]
    sums = pieces[0].astype(full)
    for d in range(1, 4):
        sums = sums + crossed(pieces[d], d, 0).astype(full)
    sums = sums.astype(low)

    corners = [pieces[1][0, 0, :16, :128]]
    partial, gain_term, bias_term = find_hidden_grad(
        table, grad_qkv, held, normed, corners
    )
    bias_term = bias_term.reshape(3, 1, half)
    nothing = jnp.zeros_like(bias_term)
    bias_term = jnp.where(
        first,
        jnp.concatenate([bias_term, nothing], 1),
        jnp.concatenate([nothing, bias_term], 1),
    )
    small = jnp.concatenate([gain_term.reshape(-1), bias_term.reshape(-1)]).reshape(16, 256)
    small = small + swap(small)

    def split(values):
        upper = lax.reduce_precision(values, 8, 7)
        return jnp.concatenate([upper.astype(low), (values - upper).astype(low)], 0)

    def joined(rows):
        return rows[-32:-16].astype(full) + rows[-16:].astype(full)

    def with_small(rows, extra_rows):
        return jnp.concatenate([rows.reshape(-1, 256), extra_rows], 0)

    extra_rows = split(small)
    total = sums[0].reshape(-1, 256).astype(full)
    for d in range(1, 4):
        arrived = crossed(with_small(sums[d], extra_rows), d, 1)
        total = total + arrived[:-32].astype(full)
        small = small + joined(arrived)
    sums = total.astype(low).reshape(8, own_rows, 256)
    repeated = jnp.broadcast_to(small.astype(low), (8, 16, 256))
    arrived = trade_z(jnp.concatenate([sums, repeated], 1))
    final = jnp.sum(arrived.astype(full), 0).astype(low)
    arrived = trade_space(jnp.broadcast_to(final, (8, own_rows + 16, 256)))
    small = jnp.sum(arrived[:4, own_rows:].astype(full), 0)
    rows = arrived[:, :own_rows]
    rows = jnp.where(
        first, rows.reshape(2, 4, own_rows, 256).swapaxes(0, 1).reshape(rows.shape), rows
    )
    others = swap(rows)
    small_got = swap(small)
    small = jnp.where(first, small, small_got).reshape(-1)
    sides = (jnp.where(first, rows, others), jnp.where(first, others, rows))
    blocks = [side[2 * i + j].astype(full) for i in range(4) for side in sides for j in range(2)]
    out_qkv = jnp.concatenate(blocks[:12], 1)
    out_proj = jnp.concatenate(blocks[12:], 1)

    grad_hidden = partial[:ROWS] + swap(partial[ROWS:])
    grad_norm = grad_hidden * ln_gain
    own_normed = normed[:ROWS]
    grad_flat = rows_g.astype(full) + inv_std[:ROWS] * (
        grad_norm
        - jnp.mean(grad_norm, -1, keepdims=True)
        - own_normed * jnp.mean(grad_norm * own_normed, -1, keepdims=True)
    )
    grad_tile = jnp.roll(
        grad_flat[:TOKENS].astype(low).reshape(inputs.shape), (SHIFT, SHIFT), (2, 3)
    )
    returned = lax.ppermute(
        grad_tile[:, WIN - SHIFT :], "space", [(i, (i + 1) % n_space) for i in range(n_space)]
    )
    grad_input = jnp.concatenate([returned, grad_tile[:, : WIN - SHIFT]], 1)
    return (grad_input, out_qkv, out_proj, small[:width], small[width:])


def solution(mesh):
    tokens = P("batch", "space", None, None, None)
    return jax.shard_map(
        per_device,
        mesh=mesh,
        in_specs=(tokens, tokens, P("space", None, None), P("batch", None), P(), P("batch", None), P()),
        out_specs=(tokens, P("batch", None), P("batch", None), P(), P()),
        check_vma=False,
    )
```

```python
import itertools
import math

import jax
import jax.numpy as jnp
from jax import lax
from jax.experimental import pallas as pl
from jax.experimental.pallas import tpu as pltpu
from jax.sharding import PartitionSpec as P

HEADS = 16
WIN = 7
SHIFT = 3
TOKENS = WIN**3
ROWS = 352
EPS = 1e-05
NEG = -1e30
BOTH = ("space", "batch")


def flat(x, y, z, c):
    return ((y // 2 * 4 + x) * 2 + c) * 16 + z * 2 + y % 2


def places():
    s = lax.axis_index("space").astype(jnp.uint32)
    b = lax.axis_index("batch").astype(jnp.uint32)
    return (s >> 1) & 3, (s >> 3) * 2 + (b & 1), b >> 1, s & 1


def route(where):
    every = itertools.product(range(4), range(4), range(8), range(2))
    return [(flat(*at), flat(*where(*at))) for at in every]


def swap(block):
    return lax.ppermute(block, BOTH, route(lambda x, y, z, c: (x, y, z, 1 - c)))


def crossed(block, d, swapped):
    def where(x, y, z, c):
        if c == swapped:
            return ((x + d) % 4, y, z, c)
        return (x, (y + d) % 4, z, c)

    return lax.ppermute(block, BOTH, route(where))


def trade_z(blocks):
    groups = [[z * 2 + low_y for z in range(8)] for low_y in range(2)]
    return lax.all_to_all(blocks, "batch", 0, 0, tiled=True, axis_index_groups=groups)


def trade_space(blocks):
    groups = [[chip * 2 + c for chip in range(8)] for c in range(2)]
    return lax.all_to_all(blocks, "space", 0, 0, tiled=True, axis_index_groups=groups)


def attention_kernel(q_ref, k_ref, v_ref, g_ref, mask_ref, attn_ref, grad_ref):
    full = jnp.float32
    size = 64
    scale = 1.0 / math.sqrt(size)
    over_rows = (((0,), (0,)), ((), ()))
    over_columns = (((1,), (1,)), ((), ()))
    mask = mask_ref[0]
    for_queries = []
    for head in range(8):
        part = slice(head * size, (head + 1) * size)
        q, k, v, g = q_ref[:, part], k_ref[:, part], v_ref[:, part], g_ref[:, part]
        scaled = q * jnp.bfloat16(scale)
        scores = lax.dot_general(k, scaled, over_columns, preferred_element_type=full) + mask
        exponent = jnp.exp(scores - jnp.max(scores, 0, keepdims=True))
        probability = exponent * (1.0 / jnp.sum(exponent, 0, keepdims=True))
        low = probability.astype(jnp.bfloat16)
        grad = lax.dot_general(v, g, over_columns, preferred_element_type=full)
        centre = jnp.sum(probability * grad, 0, keepdims=True)
        score_low = (probability * (grad - centre)).astype(jnp.bfloat16)
        attn_t = lax.dot_general(v, low, over_rows, preferred_element_type=full)
        grad_q_t = lax.dot_general(k, score_low, over_rows, preferred_element_type=full) * scale
        for_queries.append((attn_t.astype(jnp.bfloat16), grad_q_t.astype(jnp.bfloat16)))
        grad_ref[1, :, part] = (
            jnp.dot(score_low, q, preferred_element_type=full) * scale
        ).astype(jnp.bfloat16)
        grad_ref[2, :, part] = jnp.dot(low, g, preferred_element_type=full).astype(jnp.bfloat16)
    for parity in range(2):
        attn_ref[parity] = jnp.concatenate(
            [attn for attn, _ in for_queries[parity::2]], 0
        ).T
    grad_ref[0] = jnp.concatenate([grad for _, grad in for_queries], 0).T


def attend(qkv, dout, mask):
    rows, width = dout.shape
    groups = width // 512

    def columns(offset):
        return pl.BlockSpec((ROWS, 512), lambda w, j: (w, offset + j))

    work = 2 * groups * 8
    return pl.pallas_call(
        attention_kernel,
        grid=(2, groups),
        in_specs=[
            columns(0),
            columns(groups),
            columns(2 * groups),
            columns(0),
            pl.BlockSpec((1, ROWS, ROWS), lambda w, j: (w, 0, 0)),
        ],
        out_specs=[
            pl.BlockSpec((2, ROWS, 256), lambda w, j: (0, w, j)),
            pl.BlockSpec((3, ROWS, 512), lambda w, j: (0, w, j)),
        ],
        out_shape=[
            jax.ShapeDtypeStruct((2, rows, width // 2), jnp.bfloat16),
            jax.ShapeDtypeStruct((3, rows, width), jnp.bfloat16),
        ],
        cost_estimate=pl.CostEstimate(
            flops=work * 14 * ROWS * ROWS * 64 * 4,
            bytes_accessed=8 * rows * width * 2,
            transcendentals=work * ROWS * ROWS,
        ),
        compiler_params=pltpu.CompilerParams(vmem_limit_bytes=24 * 2**20),
    )(qkv, qkv, qkv, dout, mask)


SMALL = pltpu.CompilerParams(vmem_limit_bytes=2**20)
LIMIT = pltpu.CompilerParams(vmem_limit_bytes=20 * 2**20)
LARGE = pltpu.CompilerParams(vmem_limit_bytes=30 * 2**20)


def cost(flops, bytes_accessed):
    return pl.CostEstimate(flops=flops, bytes_accessed=bytes_accessed, transcendentals=0)


def follow(array, after):
    return pl.pallas_call(
        lambda *refs: None,
        in_specs=[pl.BlockSpec(memory_space=pl.ANY)] * (1 + len(after)),
        out_specs=pl.BlockSpec(memory_space=pl.ANY),
        out_shape=jax.ShapeDtypeStruct(array.shape, array.dtype),
        input_output_aliases={0: 0},
        cost_estimate=cost(0, 0),
        compiler_params=SMALL,
    )(array, *after)


SMEM = pl.BlockSpec(memory_space=pltpu.SMEM)
VMEM = pl.BlockSpec(memory_space=pltpu.VMEM)


def assemble_kernel(x_ref, g_ref, rim_ref, walls_ref, rows_x_ref, rows_g_ref, sent_ref, held_ref):
    for which, (ref, out_ref) in enumerate(((x_ref, rows_x_ref), (g_ref, rows_g_ref))):
        for i in range(WIN):
            for j in range(WIN):
                across = (j + SHIFT) % WIN
                if i + SHIFT < WIN:
                    line = ref[0, i + SHIFT, across]
                else:
                    line = rim_ref[0, which * SHIFT + i + SHIFT - WIN, across]
                line = line.astype(jnp.float32)
                row = (i * WIN + j) * WIN
                held_ref[row : row + WIN - SHIFT] = line[SHIFT:]
                held_ref[row + WIN - SHIFT : row + WIN] = line[:SHIFT]
        held_ref[TOKENS:] = jnp.zeros((ROWS - TOKENS, held_ref.shape[1]), jnp.float32)
        out_ref[...] = held_ref[...].astype(jnp.bfloat16)
    held_ref[TOKENS : TOKENS + 1] = walls_ref[...].astype(jnp.float32)
    sent_ref[...] = held_ref[...].astype(jnp.bfloat16)


def assemble(inputs, grad_out, rims, walls_row):
    width = inputs.shape[-1]
    return pl.pallas_call(
        assemble_kernel,
        in_specs=[VMEM] * 4,
        out_specs=[VMEM] * 3,
        out_shape=[jax.ShapeDtypeStruct((ROWS, width), jnp.bfloat16)] * 3,
        scratch_shapes=[pltpu.VMEM((ROWS, width), jnp.float32)],
        cost_estimate=cost(0, 0),
        compiler_params=LIMIT,
    )(inputs, grad_out, rims, walls_row)


def norm_kernel(own_ref, got_ref, gain_ref, normed_ref, by_ref, t_ref, inv_ref):
    for i, ref in enumerate((own_ref, got_ref)):
        rows = ref[...].astype(jnp.float32)
        part = slice(i * ROWS, (i + 1) * ROWS)
        centred = rows - jnp.mean(rows, -1, keepdims=True)
        variance = jnp.mean(centred * centred, -1, keepdims=True)
        inv_std = 1.0 / jnp.sqrt(variance + EPS)
        normed = centred * inv_std
        hidden = (normed * gain_ref[...]).astype(jnp.bfloat16)
        normed_ref[part, :] = normed
        inv_ref[part, :] = inv_std
        for z in range(8):
            for low_y in range(2):
                column = (z * 2 + low_y) * 64
                by_ref[low_y, part, z * 64 : (z + 1) * 64] = hidden[:, column : column + 64]
    for low_y in range(2):
        t_ref[low_y] = by_ref[low_y].T


def normalise(own, got, gain):
    rows, width = own.shape
    return pl.pallas_call(
        norm_kernel,
        in_specs=[VMEM] * 3,
        out_specs=[VMEM] * 4,
        out_shape=[
            jax.ShapeDtypeStruct((2 * rows, width), jnp.float32),
            jax.ShapeDtypeStruct((2, 2 * rows, width // 2), jnp.bfloat16),
            jax.ShapeDtypeStruct((2, width // 2, 2 * rows), jnp.bfloat16),
            jax.ShapeDtypeStruct((2 * rows, 1), jnp.float32),
        ],
        cost_estimate=cost(0, 0),
        compiler_params=LIMIT,
    )(own, got, gain)


def collect_kernel(spots_ref, w0, w1, w2, w3, held_ref, kept_ref, sent_ref, sems):
    core = spots_ref[16]
    copies = [
        pltpu.make_async_copy(ref, held_ref.at[pl.ds(4 * d, 4)], sems.at[d])
        for d, ref in enumerate((w0, w1, w2, w3))
    ]
    for copy in copies:
        copy.start()
    for copy in copies:
        copy.wait()
    for i in range(4):
        spot = spots_ref[12 + i]
        kept_ref[i] = held_ref[spot, pl.ds(pl.multiple_of(core * 256, 256), 256), :]
        sent_ref[i] = held_ref[spot, pl.ds(pl.multiple_of((1 - core) * 256, 256), 256), :]


def collect(spots, weights):
    anywhere = pl.BlockSpec(memory_space=pl.ANY)
    return pl.pallas_call(
        collect_kernel,
        in_specs=[SMEM] + [anywhere] * 4,
        out_specs=[VMEM] * 3,
        out_shape=[jax.ShapeDtypeStruct((16, 512, 256), jnp.bfloat16)]
        + [jax.ShapeDtypeStruct((4, 256, 256), jnp.bfloat16)] * 2,
        scratch_shapes=[pltpu.SemaphoreType.DMA((4,))],
        cost_estimate=cost(0, 8 * 2**20),
        compiler_params=LIMIT,
    )(spots, *weights)


def project_kernel(spots_ref, hidden_ref, held_ref, bias_ref, out_ref):
    for block in range(6):
        total = bias_ref[block]
        for low_y in range(2):
            total = total + jnp.dot(
                hidden_ref[low_y],
                held_ref[spots_ref[low_y * 6 + block]],
                preferred_element_type=jnp.float32,
            )
        out_ref[:, block * 256 : (block + 1) * 256] = total.astype(jnp.bfloat16)


def project(spots, hidden, held, biases):
    rows = hidden.shape[1]
    return pl.pallas_call(
        project_kernel,
        in_specs=[SMEM] + [VMEM] * 3,
        out_specs=VMEM,
        out_shape=jax.ShapeDtypeStruct((rows, 1536), jnp.bfloat16),
        cost_estimate=cost(2 * rows * 1024 * 1536, 8 * 2**20),
        compiler_params=LIMIT,
    )(spots, hidden, held, biases)


def dout_kernel(grad_ref, kept_ref, got_ref, out_ref):
    for low_y in range(2):
        total = 0.0
        for i in range(4):
            ref = kept_ref if i < 2 else got_ref
            total = total + lax.dot_general(
                grad_ref[:, i * 256 : (i + 1) * 256],
                ref[low_y * 2 + i % 2],
                (((1,), (1,)), ((), ())),
                preferred_element_type=jnp.float32,
            )
        total = total.astype(jnp.bfloat16)
        for i in range(4):
            head = 2 * i + low_y
            out_ref[:, head * 64 : (head + 1) * 64] = total[:, i * 64 : (i + 1) * 64]


def find_dout(grads, kept, got):
    rows = grads.shape[0]
    return pl.pallas_call(
        dout_kernel,
        in_specs=[VMEM] * 3,
        out_specs=VMEM,
        out_shape=jax.ShapeDtypeStruct((rows, 512), jnp.bfloat16),
        cost_estimate=cost(2 * rows * 1024 * 512, 4 * 2**20),
        compiler_params=LIMIT,
    )(grads, kept, got)


def terms_kernel(spots_ref, left_ref, right_ref, out_ref):
    for low_y in range(2):
        left = left_ref[low_y]
        for block in range(6):
            right = right_ref[block // 2, :, block % 2 * 256 : (block % 2 + 1) * 256]
            out_ref[spots_ref[low_y * 6 + block]] = jnp.dot(
                left, right, preferred_element_type=jnp.float32
            ).astype(jnp.bfloat16)


def find_terms(spots, hidden_t, grad_qkv):
    _, half, rows = hidden_t.shape
    return pl.pallas_call(
        terms_kernel,
        in_specs=[SMEM] + [VMEM] * 2,
        out_specs=VMEM,
        out_shape=jax.ShapeDtypeStruct((16, half, 256), jnp.bfloat16),
        cost_estimate=cost(2 * rows * half * 3072, 8 * 2**20),
        compiler_params=LIMIT,
    )(spots, hidden_t, grad_qkv)


def last_terms_kernel(spots_ref, attn_ref, got_ref, grads_ref, terms_ref, out_ref):
    core = spots_ref[16]
    rows = grads_ref.shape[0] // 2
    grads = grads_ref[...]

    def product(left, right):
        return lax.dot_general(
            left, right, (((0,), (0,)), ((), ())), preferred_element_type=jnp.float32
        )

    out_ref[0, pl.ds(pl.multiple_of(core * 256, 256), 256), :] = product(
        attn_ref[0], grads
    ).astype(jnp.bfloat16)
    out_ref[0, pl.ds(pl.multiple_of((1 - core) * 256, 256), 256), :] = (
        product(got_ref[0, :rows], grads[rows:]) + product(got_ref[0, rows:], grads[:rows])
    ).astype(jnp.bfloat16)


def add_last_terms(spots, attn, got, grads, terms):
    _, rows, width = attn.shape
    return pl.pallas_call(
        last_terms_kernel,
        grid_spec=pltpu.PrefetchScalarGridSpec(
            num_scalar_prefetch=1,
            grid=(4,),
            in_specs=[
                pl.BlockSpec((1, rows, width), lambda i, spots: (i // 2, 0, 0)),
                pl.BlockSpec((1, rows, width), lambda i, spots: (i // 2, 0, 0)),
                pl.BlockSpec((rows, 256), lambda i, spots: (0, i % 2)),
                pl.BlockSpec(memory_space=pl.ANY),
            ],
            out_specs=pl.BlockSpec((1, 512, 256), lambda i, spots: (spots[12 + i], 0, 0)),
        ),
        out_shape=jax.ShapeDtypeStruct(terms.shape, terms.dtype),
        input_output_aliases={4: 0},
        cost_estimate=cost(2 * rows * 1024 * 512, 4 * 2**20),
        compiler_params=LIMIT,
    )(spots, attn, got, grads, terms)


def hidden_grad_kernel(spots_ref, grad_ref, held_ref, normed_ref, *rest):
    out_ref, gain_ref, bias_ref = rest[-3:]
    for i in range(3):
        bias_ref[i] = jnp.sum(grad_ref[i].astype(jnp.float32), 0, keepdims=True)
    for low_y in range(2):
        total = 0.0
        for block in range(6):
            total = total + lax.dot_general(
                grad_ref[block // 2, :, block % 2 * 256 : (block % 2 + 1) * 256],
                held_ref[spots_ref[low_y * 6 + block]],
                (((1,), (1,)), ((), ())),
                preferred_element_type=jnp.float32,
            )
        for z in range(8):
            column = (z * 2 + low_y) * 64
            out_ref[:, column : column + 64] = total[:, z * 64 : (z + 1) * 64]
    gain_ref[...] = jnp.sum(out_ref[...] * normed_ref[...], 0, keepdims=True)


def find_hidden_grad(spots, grad_qkv, held, normed, after):
    rows, width = normed.shape
    return pl.pallas_call(
        hidden_grad_kernel,
        in_specs=[SMEM] + [VMEM] * 3 + [pl.BlockSpec(memory_space=pl.ANY)] * len(after),
        out_specs=[VMEM] * 3,
        out_shape=[
            jax.ShapeDtypeStruct((rows, width), jnp.float32),
            jax.ShapeDtypeStruct((1, width), jnp.float32),
            jax.ShapeDtypeStruct((3, 1, width // 2), jnp.float32),
        ],
        cost_estimate=cost(2 * rows * width * 1536, 14 * 2**20),
        compiler_params=LARGE,
    )(spots, grad_qkv, held, normed, *after)


def per_device(inputs, grad_out, fluid, w_qkv, qkv_bias, w_proj, ln_gain):
    full, low = jnp.float32, jnp.bfloat16
    width = w_proj.shape[1]
    half = width // 2
    x, y, z, core = places()
    first = core == 0
    own_rows = w_qkv.shape[0]
    n_space = lax.axis_size("space")
    zero = jnp.uint32(0)

    def block_of(x, y):
        return jnp.where(first, x * 2 + (y >> 1), (y >> 1) * 4 + x)

    inner_at, outer_at = jnp.where(first, y, x), jnp.where(first, x, y)
    low_y = jnp.array([i // 6 for i in range(12)] + [i // 2 for i in range(4)], jnp.uint32)
    block = jnp.array([i % 6 for i in range(12)] + [6 + i % 2 for i in range(4)], jnp.uint32)
    block, side = block >> 1, block & 1
    outer_to = jnp.where(first, block, low_y + (block & 2))
    inner_to = jnp.where(first, low_y + 2 * side, (block & 1) * 2 + side)
    spots = ((outer_to - outer_at) & 3) * 4 + ((inner_to - inner_at) & 3)
    spots = jnp.concatenate([spots, core.reshape(1)]).astype(jnp.int32)
    table = ((outer_at - outer_to) & 3) * 4 + ((inner_at - inner_to) & 3)
    table = jnp.concatenate([table, core.reshape(1)]).astype(jnp.int32)

    def back(block):
        return lax.ppermute(block, "space", [((i + 1) % n_space, i) for i in range(n_space)])

    walls_plane = jnp.pad(
        fluid[:SHIFT].transpose(1, 2, 0).astype(low), ((0, 0), (0, 0), (0, width - SHIFT))
    )
    rims = back(
        jnp.concatenate([inputs[:, :SHIFT], grad_out[:, :SHIFT], walls_plane[None, None]], 1)
    )
    qkv_parts = w_qkv.reshape(own_rows, 3, 2, half)
    mine = jnp.concatenate(
        [jnp.where(first, qkv_parts[:, i, 0], qkv_parts[:, i, 1]) for i in range(3)]
        + [jnp.where(first, w_proj[:, :half], w_proj[:, half:])],
        1,
    )
    share = lax.dynamic_slice(mine, (zero, block_of(x, y) * 256), (own_rows, 256))
    lined = trade_z(jnp.broadcast_to(share, (8, own_rows, 256)))
    arrived = [crossed(lined, d, 1) for d in range(1, 4)]
    rims = follow(rims, (arrived[0][0, :16, :128],))
    quarters = jnp.stack([lined] + arrived)
    rim_f = rims[0, 2 * SHIFT, :, :, :SHIFT].transpose(2, 0, 1).astype(fluid.dtype)
    tile_f = jnp.roll(jnp.concatenate([fluid[SHIFT:], rim_f], 0), (-SHIFT, -SHIFT), (1, 2))
    walls_row = jnp.pad(tile_f.reshape(1, -1).astype(low), ((0, 0), (0, width - TOKENS)))
    rows_x, rows_g, sent_g = assemble(inputs, grad_out, rims, walls_row)
    normed, hidden_by, hidden_t, inv_std = normalise(
        rows_x, swap(rows_x), ln_gain.reshape(1, width)
    )
    got_g = swap(sent_g)
    other_f = got_g[TOKENS, :TOKENS].astype(fluid.dtype)
    extra = ((0, ROWS - TOKENS), (0, 0))
    grads = jnp.concatenate([rows_g, jnp.pad(got_g[:TOKENS], extra)], 0)
    grads_own_first = jnp.where(
        first, grads, jnp.concatenate([grads[:, half:], grads[:, :half]], 1)
    )

    steps = jnp.arange(WIN, dtype=jnp.int32)
    inner = jnp.where(steps < WIN - SHIFT, 1, 2).astype(jnp.int32)
    last_pair = (x == 3) & (y >= 2)

    def masked(walls, is_last):
        along = jnp.where(is_last, inner, 0)
        labels = along[:, None, None] * 9 + inner[None, :, None] * 3 + inner[None, None, :]
        labels = jnp.pad(labels.reshape(-1), (0, ROWS - TOKENS), constant_values=-1)
        open_keys = jnp.pad(walls.reshape(-1) == 1, (0, ROWS - TOKENS))
        allowed = (labels[:, None] == labels[None, :]) & (
            open_keys[:, None] | jnp.eye(ROWS, dtype=bool)
        )
        return jnp.where(allowed, 0.0, NEG).astype(full)

    mask = jnp.stack([masked(tile_f, last_pair & ~first), masked(other_f, last_pair & first)])

    biases = qkv_bias.reshape(3, 2, half)
    biases = jnp.where(first, biases[:, 0], biases[:, 1]).reshape(6, 1, 256)
    weights = [quarters] + [crossed(quarters, d, 0) for d in range(1, 4)]
    weights[1] = follow(
        weights[1], (hidden_t, hidden_by, normed, mask, grads_own_first, biases, table, spots)
    )
    weights = [piece.reshape(4, half, 256) for piece in weights]
    held, kept, sent = collect(table, weights)
    got = swap(sent)
    qkv = project(table, hidden_by, held, biases)
    dout = find_dout(grads_own_first, kept, got)
    attn, grad_qkv = attend(qkv, dout, mask)

    terms = add_last_terms(
        spots, attn, swap(attn), grads_own_first, find_terms(spots, hidden_t, grad_qkv)
    )
    pieces = terms.reshape(4, 4, 8, own_rows, 256)
    pieces = [pieces[d] for d in range(4)]
    sums = pieces[0].astype(full)
    for d in range(1, 4):
        sums = sums + crossed(pieces[d], d, 0).astype(full)
    sums = sums.astype(low)

    corners = [pieces[1][0, 0, :16, :128]]
    partial, gain_term, bias_term = find_hidden_grad(
        table, grad_qkv, held, normed, corners
    )
    bias_term = bias_term.reshape(3, 1, half)
    nothing = jnp.zeros_like(bias_term)
    bias_term = jnp.where(
        first,
        jnp.concatenate([bias_term, nothing], 1),
        jnp.concatenate([nothing, bias_term], 1),
    )
    small = jnp.concatenate([gain_term.reshape(-1), bias_term.reshape(-1)]).reshape(16, 256)
    small = small + swap(small)

    def split(values):
        upper = lax.reduce_precision(values, 8, 7)
        return jnp.concatenate([upper.astype(low), (values - upper).astype(low)], 0)

    def joined(rows):
        return rows[-32:-16].astype(full) + rows[-16:].astype(full)

    def with_small(rows, extra_rows):
        return jnp.concatenate([rows.reshape(-1, 256), extra_rows], 0)

    extra_rows = split(small)
    total = sums[0].reshape(-1, 256).astype(full)
    for d in range(1, 4):
        arrived = crossed(with_small(sums[d], extra_rows), d, 1)
        total = total + arrived[:-32].astype(full)
        small = small + joined(arrived)
    sums = total.astype(low).reshape(8, own_rows, 256)
    repeated = jnp.broadcast_to(small.astype(low), (8, 16, 256))
    arrived = trade_z(jnp.concatenate([sums, repeated], 1))
    final = jnp.sum(arrived.astype(full), 0).astype(low)
    arrived = trade_space(jnp.broadcast_to(final, (8, own_rows + 16, 256)))
    small = jnp.sum(arrived[:4, own_rows:].astype(full), 0)
    rows = arrived[:, :own_rows]
    rows = jnp.where(
        first, rows.reshape(2, 4, own_rows, 256).swapaxes(0, 1).reshape(rows.shape), rows
    )
    others = swap(rows)
    small_got = swap(small)
    small = jnp.where(first, small, small_got).reshape(-1)
    sides = (jnp.where(first, rows, others), jnp.where(first, others, rows))
    blocks = [side[2 * i + j].astype(full) for i in range(4) for side in sides for j in range(2)]
    out_qkv = jnp.concatenate(blocks[:12], 1)
    out_proj = jnp.concatenate(blocks[12:], 1)

    grad_hidden = partial[:ROWS] + swap(partial[ROWS:])
    grad_norm = grad_hidden * ln_gain
    own_normed = normed[:ROWS]
    grad_flat = rows_g.astype(full) + inv_std[:ROWS] * (
        grad_norm
        - jnp.mean(grad_norm, -1, keepdims=True)
        - own_normed * jnp.mean(grad_norm * own_normed, -1, keepdims=True)
    )
    grad_tile = jnp.roll(
        grad_flat[:TOKENS].astype(low).reshape(inputs.shape), (SHIFT, SHIFT), (2, 3)
    )
    returned = lax.ppermute(
        grad_tile[:, WIN - SHIFT :], "space", [(i, (i + 1) % n_space) for i in range(n_space)]
    )
    grad_input = jnp.concatenate([returned, grad_tile[:, : WIN - SHIFT]], 1)
    return (grad_input, out_qkv, out_proj, small[:width], small[width:])


def solution(mesh):
    tokens = P("batch", "space", None, None, None)
    return jax.shard_map(
        per_device,
        mesh=mesh,
        in_specs=(tokens, tokens, P("space", None, None), P("batch", None), P(), P("batch", None), P()),
        out_specs=(tokens, P("batch", None), P("batch", None), P(), P()),
        check_vma=False,
    )
```
